128 devices in a mesh: blk: 16 (over y_hi, x, core), grp: 8 (over y_lo, z).
Axes of the slice: x: 4, y: 4 (y_hi: 2, y_lo: 2; y = y_hi * 2 + y_lo), z: 4, core: 2. Of those that a mesh axis runs over, the one named last changes fastest.
Arguments:
- particles: bfloat16 [12288, 4096], P(('blk', 'grp')), may hold values from -24 to 24
- references: bfloat16 [1536, 4096], P(('blk', 'grp')), may hold values from -6 to 6
- candidates: int32 [12288, 4], P(('blk', 'grp')), may hold values from 0 to 191, as said below
- shifts: int32 [9, 2], replicated, may hold values from -4 to 4, as said below
- class_order: int32 [192], replicated, may hold values from 0 to 191, each once
Outputs:
- new_refs: float32 [192, 4096], P('blk', 'grp')
The draws below stay inside these ranges and needn't reach their ends.
Inputs may be any that keep to these rules, and one draw needn't show every extreme that they name: Each particle's 4 candidates are different classes. `shifts`: the first translation is zero; some translation is (4, -4).
All inputs are finite; a program needn't handle non-finite values.
Results may differ from the reference program's by a relative error of at most 0.0076.
Values may be sent and summed in bfloat16 or wider, within the bound.
A program may use at most 128 MiB of HBM per device.

```python
import jax
import jax.numpy as jnp
from jax import lax

K = 4096
BOX = 128
CLS = 192
ROT = 8
REFS = 1536
TRANS = 9
CAND = 4
PART_DEV = 96
PARTICLES = 12288
N_BLK = 16
N_GRP = 8


def class_lists(key):
    inner = jax.random.fold_in(key, 101)
    first, second = jax.random.split(inner)
    start = jax.random.randint(first, (PARTICLES, 1), 0, CLS)
    stride = jax.random.randint(second, (PARTICLES, 1), 1, CLS // CAND)
    return ((start + jnp.arange(CAND)[None, :] * stride) % CLS).astype(jnp.int32)


def base_images(key):
    inner = jax.random.fold_in(key, 202)
    return jnp.clip(jax.random.normal(inner, (REFS, K), jnp.float32), -6.0, 6.0)


def draw_candidates(key, part):
    return class_lists(key)


def draw_references(key, part):
    return base_images(key).astype(jnp.bfloat16)


def draw_particles(key, part):
    key = jax.random.fold_in(key, 3)
    first = jax.random.fold_in(key, 0)
    values = jnp.clip(jax.random.normal(first, (PARTICLES, K), jnp.float32), -6.0, 6.0)
    return values.astype(jnp.bfloat16)


def draw_shifts(key, part):
    key = jax.random.fold_in(key, 5)
    moves = jax.random.randint(key, (TRANS, 2), -4, 5)
    moves = moves.at[0].set(jnp.array([0, 0], jnp.int32))
    moves = moves.at[1].set(jnp.array([4, -4], jnp.int32))
    return moves.astype(jnp.int32)


def setup_inputs(seed: int = 0) -> dict:
    arg_keys = jax.random.split(jax.random.key(seed), 6)
    particles = draw_particles(jax.random.fold_in(arg_keys[5], 71), 0)
    references = draw_references(jax.random.fold_in(arg_keys[5], 71), 0)
    candidates = draw_candidates(jax.random.fold_in(arg_keys[5], 71), 0)
    shifts = draw_shifts(jax.random.fold_in(arg_keys[5], 71), 0)
    class_order = jax.random.permutation(arg_keys[4], CLS).astype(jnp.int32)
    return {"particles": particles, "references": references, "candidates": candidates, "shifts": shifts, "class_order": class_order}


score_scale = 0.05


def shift_block(block, shifts):
    half_width = block.shape[1] // 2
    index = jnp.arange(half_width, dtype=jnp.int32)
    freq_x = (index % (BOX // 2)).astype(jnp.float32)
    freq_y = (index // (BOX // 2)).astype(jnp.float32)
    moves = shifts.astype(jnp.float32)
    angle = 2.0 * jnp.pi * (moves[:, 0:1] * freq_x[None, :] + moves[:, 1:2] * freq_y[None, :]) / BOX
    cosine = jnp.cos(angle)[None]
    sine = jnp.sin(angle)[None]
    real_part = block[:, :half_width].astype(jnp.float32)[:, None, :]
    imag_part = block[:, half_width:].astype(jnp.float32)[:, None, :]
    new_real = real_part * cosine - imag_part * sine
    new_imag = real_part * sine + imag_part * cosine
    return jnp.concatenate([new_real, new_imag], axis=2).astype(jnp.bfloat16)


def reference(particles, references, candidates, shifts, class_order):
    count_blocks = N_BLK * N_GRP
    width = particles.shape[1]
    half_norm = 0.5 * jnp.sum(jnp.square(references.astype(jnp.float32)), axis=1)
    ref_class = jnp.arange(REFS, dtype=jnp.int32) // ROT
    blocks = particles.reshape(count_blocks, PART_DEV, width)
    lists = candidates.reshape(count_blocks, PART_DEV, CAND)

    def step(carry, item):
        sums, totals = carry
        block, chosen = item
        shifted = shift_block(block, shifts)
        flat = shifted.reshape(PART_DEV * TRANS, width)
        raw = jnp.dot(flat, references.T, preferred_element_type=jnp.float32)
        logits = (score_scale * (raw - half_norm[None, :])).reshape(PART_DEV, TRANS, REFS)
        allowed = jnp.any(chosen[:, :, None] == ref_class[None, None, :], axis=1)
        logits = jnp.where(allowed[:, None, :], logits, -1e30)
        top = jnp.max(logits, axis=(1, 2), keepdims=True)
        expo = jnp.exp(logits - top)
        weights = expo / jnp.sum(expo, axis=(1, 2), keepdims=True)
        class_weight = weights.reshape(PART_DEV, TRANS, CLS, ROT).sum(axis=3)
        totals = totals + class_weight.sum(axis=(0, 1))
        rounded = class_weight.astype(jnp.bfloat16).reshape(PART_DEV * TRANS, CLS)
        sums = sums + jnp.dot(rounded.T, flat, preferred_element_type=jnp.float32)
        return (sums, totals), None

    start = (jnp.zeros((CLS, width), jnp.float32), jnp.zeros((CLS,), jnp.float32))
    (sums, totals), _ = lax.scan(step, start, (blocks, lists))
    averaged = sums / (totals[:, None] + 1.0)
    return averaged[class_order]
```

```python
import math

import jax
import jax.numpy as jnp
from jax import lax
from jax.experimental import pallas as pl
from jax.experimental.pallas import tpu as pltpu
from jax.sharding import PartitionSpec as P

BOX = 128
ROT = 8
SCALE = 0.05
HALF = 512
PART = 96
TRANS = 9
ROWS = 896
CLS = 192
REFS = 1536
ORDER = (2, 1, 3, 0)
NT = (((1,), (1,)), ((), ()))
F32 = jnp.float32
BF16 = jnp.bfloat16


def pos_of(offset):
    return ORDER.index(offset % 4)


def kernel(
    parts, refs_in, cand_in, shifts, order, out,
    stage, stage32, refs, pb, sh, cb, hn, e_out, e_in, wb, wt, msg, fin,
    st_send, st_recv, pt_send, pt_recv, cd_send, cd_recv,
    ag_send, ag_recv, sb_send, sb_recv, rs_send, rs_recv, ww_send, ww_recv, fn_send, fn_recv,
):
    b = lax.axis_index("blk")
    g = lax.axis_index("grp")
    c = b % 2
    x = (b // 2) % 4
    y = (b // 8) * 2 + g // 4
    z = g % 4

    def dev(x_, y_, c_, z_):
        return (((y_ // 2) * 4 + x_) * 2 + c_, (y_ % 2) * 4 + z_)

    def remote(src, dst, ssem, rsem, device):
        return pltpu.make_async_remote_copy(
            src_ref=src, dst_ref=dst, send_sem=ssem, recv_sem=rsem,
            device_id=device, device_id_type=pl.DeviceIdType.MESH)

    def zdev(delta):
        return dev(x, y, c, (z + delta) % 4)

    barrier = pltpu.get_barrier_semaphore()
    me32 = (x * 4 + y) * 2 + c

    def greet(k, _):
        i = (me32 + k) % 32
        pl.semaphore_signal(barrier, inc=1, device_id=dev(i // 8, (i // 2) % 4, i % 2, z),
                            device_id_type=pl.DeviceIdType.MESH)
        return 0

    lax.fori_loop(1, 32, greet, 0)
    for dz in (1, 2, 3):
        for dc in (0, 1):
            pl.semaphore_signal(barrier, inc=1, device_id=dev(x, y, (c + dc) % 2, (z + dz) % 4),
                                device_id_type=pl.DeviceIdType.MESH)
    pl.semaphore_wait(barrier, 37)

    def stage_copy(dc, dz):
        k = dc * 4 + dz
        c_ = (c + dc) % 2
        z_ = (z + dz) % 4
        cols = pl.ds(pl.multiple_of(c_ * 2048 + z_ * 512, 512), 512)
        return remote(refs_in.at[:, cols], stage.at[c * 4 + z], st_send.at[k], st_recv.at[k],
                      dev(x, y, c_, z_))

    stage_offsets = [(dc, dz) for dz in (2, 1, 3, 0) for dc in (0, 1) if dc or dz]
    for dc, dz in stage_offsets:
        stage_copy(dc, dz).start()
    own_cols = pl.ds(pl.multiple_of(c * 2048 + z * 512, 512), 512)
    own_stage = pltpu.make_async_copy(refs_in.at[:, own_cols], stage.at[c * 4 + z], st_recv.at[0])
    own_stage.start()

    def part_copy(dz, h):
        z_ = (z + dz) % 4
        cols = pl.ds(pl.multiple_of(h * 2048 + z_ * 512, 512), 512)
        p = pos_of(-dz)
        return remote(parts.at[:, cols], pb.at[p, h], pt_send.at[p * 2 + h], pt_recv.at[p * 2 + h], zdev(dz))

    def cand_copy(dz):
        p = pos_of(-dz)
        return remote(cand_in, cb.at[p], cd_send.at[p], cd_recv.at[p], zdev(dz))

    for dz in (1, 3, 2):
        cand_copy(dz).start()
    for dz in (1, 3, 2):
        for h in (0, 1):
            part_copy(dz, h).start()
    own_parts = []
    for h in (0, 1):
        cols = pl.ds(pl.multiple_of(h * 2048 + z * 512, 512), 512)
        own = pltpu.make_async_copy(parts.at[:, cols], pb.at[3, h], pt_recv.at[6 + h])
        own.start()
        own_parts.append(own)
    own_cand = pltpu.make_async_copy(cand_in, cb.at[3], cd_recv.at[3])
    own_cand.start()

    for dc, dz in stage_offsets:
        stage_copy(dc, dz).wait_recv()
    own_stage.wait()
    for i in range(8):
        stage32[i * 12:(i + 1) * 12, :] = stage[i].astype(F32)

    def block_rows(x_, y_):
        return pl.ds(pl.multiple_of((x_ * 4 + y_) * 96, 96), 96)

    refs[c, block_rows(x, y), :] = stage32[...].astype(BF16)

    def at(a, b_):
        dx = a * (1 - c) + b_ * c
        dy = b_ * (1 - c) + a * c
        return (x + dx) % 4, (y + dy) % 4

    def ref_block(a, b_):
        x_, y_ = at(a, b_)
        return refs.at[c, block_rows(x_, y_), :]

    def first_send(k):
        x_, y_ = at(k, 0)
        block = ref_block(0, 0)
        return remote(block, block, ag_send.at[k], ag_recv.at[((-k) % 4) * 4], dev(x_, y_, c, z))

    def second_send(a, k):
        x_, y_ = at(0, k)
        block = ref_block(a, 0)
        return remote(block, block, ag_send.at[3 + a * 3 + k], ag_recv.at[a * 4 + (-k) % 4], dev(x_, y_, c, z))

    def recv_block(a, b_):
        block = ref_block(a, b_)
        remote(block, block, ag_send.at[0], ag_recv.at[a * 4 + b_], dev(x, y, 1 - c, z)).wait_recv()

    def sib_copy(a, b_):
        block = ref_block(a, b_)
        return remote(block, block, sb_send.at[a * 4 + b_], sb_recv.at[a * 4 + b_], dev(x, y, 1 - c, z))

    for k in (2, 1, 3):
        first_send(k).start()
    for k in (2, 1, 3):
        second_send(0, k).start()
    sib_copy(0, 0).start()

    def shift_tables():
        index = lax.broadcasted_iota(jnp.int32, (16, HALF), 1) + z * HALF
        fx = index % (BOX // 2)
        fy = index // (BOX // 2)
        moves = shifts[...]
        turns = (moves[:, 0:1] * fx + moves[:, 1:2] * fy) & (BOX - 1)
        angle = turns.astype(F32) * (2.0 * math.pi / BOX)
        return jnp.cos(angle), jnp.sin(angle)

    cosine, sine = shift_tables()

    def shift_block(p):
        base = p * ROWS
        sh[base + TRANS * PART:base + ROWS, :] = jnp.zeros((ROWS - TRANS * PART, 2 * HALF), BF16)
        for t in range(TRANS):
            for r in range(0, PART, 16):
                re = pb[p, 0, r:r + 16, :].astype(F32)
                im = pb[p, 1, r:r + 16, :].astype(F32)
                co = cosine[t:t + 1, :]
                si = sine[t:t + 1, :]
                row = base + t * PART + r
                sh[row:row + 16, 0:HALF] = (re * co - im * si).astype(BF16)
                sh[row:row + 16, HALF:2 * HALF] = (re * si + im * co).astype(BF16)

    for a in (1, 3, 2):
        recv_block(a, 0)
        for k in (2, 1, 3):
            second_send(a, k).start()
        sib_copy(a, 0).start()
    for own in own_parts:
        own.wait()
    own_cand.wait()
    shift_block(3)
    for b_ in (1, 3, 2):
        recv_block(0, b_)
        sib_copy(0, b_).start()
    for dz in (1, 3, 2):
        for h in (0, 1):
            part_copy(dz, h).wait_recv()
        cand_copy(dz).wait_recv()
        shift_block(pos_of(-dz))
        for a in (dz,):
            for b_ in (1, 3, 2):
                recv_block(a, b_)
                sib_copy(a, b_).start()
    for a in range(4):
        for b_ in range(4):
            sib_copy(a, b_).wait_recv()

    def norms(i, _):
        rows = pl.ds(pl.multiple_of(i * 96, 96), 96)
        acc = jnp.zeros((96, 128), F32)
        for h in (0, 1):
            for j in range(HALF // 128):
                v = refs[h, rows, j * 128:(j + 1) * 128].astype(F32)
                acc = acc + v * v
        hn[rows, :] = jnp.broadcast_to(0.5 * jnp.sum(acc, axis=1, keepdims=True), (96, 128))
        return 0

    lax.fori_loop(0, 16, norms, 0)

    def rs_copy(p):
        return remote(e_out.at[p], e_in.at[p], rs_send.at[p], rs_recv.at[p], zdev(ORDER[p]))

    def class_at(i):
        q, rest = divmod(i, 6)
        x_, y_, c_ = q // 8, (q // 2) % 4, q % 2
        return ((((y_ // 2) * 4 + x_) * 2 + c_) * 2 + y_ % 2) * 6 + rest

    def scores(n, _):
        off = pl.multiple_of(n * 256, 256)
        chosen = []
        for s in range(4):
            chosen.append([])
        for l in range(2):
            tile = n * 2 + l
            block = tile // 7
            lane = pl.multiple_of((tile % 7) * 128, 128)
            for s in range(4):
                chosen[s].append(jnp.broadcast_to(cb[block, s:s + 1, pl.ds(lane, 128)], (8, 128)))
        raw = (
            lax.dot_general(refs[0], sh[pl.ds(off, 256), 0:HALF], NT, preferred_element_type=F32)
            + lax.dot_general(refs[1], sh[pl.ds(off, 256), HALF:2 * HALF], NT, preferred_element_type=F32)
        )
        acc = [[jnp.zeros((8, 128), F32) for _ in range(2)] for _ in range(4)]
        for i in range(CLS):
            norm = hn[i * 8:i * 8 + 8, :]
            for l in range(2):
                v = raw[i * 8:i * 8 + 8, l * 128:l * 128 + 128] - norm
                for s in range(4):
                    acc[s][l] = jnp.where(chosen[s][l] == class_at(i), v, acc[s][l])
        for l in range(2):
            tile = n * 2 + l
            block = tile // 7
            lane = pl.multiple_of((tile % 7) * 128, 128)
            for s in range(4):
                e_out[block, s * 8:s * 8 + 8, pl.ds(lane, 128)] = acc[s][l]
        for p, last in ((0, 3), (1, 6), (2, 10)):
            @pl.when(n == last)
            def _():
                rs_copy(p).start()
        return 0

    lax.fori_loop(0, 14, scores, 0)

    for p in range(3):
        rs_copy(p).wait_recv()
    logits = SCALE * (e_out[3] + e_in[0] + e_in[1] + e_in[2])
    by_move = [logits[:, t * PART:(t + 1) * PART] for t in range(TRANS)]
    top = by_move[0]
    for t in range(1, TRANS):
        top = jnp.maximum(top, by_move[t])
    top = jnp.max(top, axis=0, keepdims=True)
    expo = [jnp.exp(v - top) for v in by_move]
    total = expo[0]
    for t in range(1, TRANS):
        total = total + expo[t]
    total = jnp.sum(total, axis=0, keepdims=True)
    pieces = []
    for t in range(TRANS):
        weight = expo[t] / total
        rows = [jnp.sum(weight[s * 8:s * 8 + 8, :], axis=0, keepdims=True) for s in range(4)]
        pieces.append(jnp.concatenate(rows + [jnp.zeros((4, PART), F32)], axis=0))
    pieces.append(jnp.zeros((8, ROWS - TRANS * PART), F32))
    wb[3] = jnp.concatenate(pieces, axis=1)

    def weight_copy(dz):
        p = pos_of(-dz)
        return remote(wb.at[3], wb.at[p], ww_send.at[p], ww_recv.at[p], zdev(dz))

    for dz in (2, 1, 3):
        weight_copy(dz).start()
    for dz in (2, 1, 3):
        weight_copy(dz).wait_recv()

    def spread(n, total_acc):
        block = n // 7
        lane = pl.multiple_of((n % 7) * 128, 128)
        wide = pl.multiple_of(n * 128, 128)
        result = []
        for r in range(0, 256, 16):
            rows = jnp.broadcast_to(order[r:r + 16, :], (16, 128))
            acc = jnp.zeros((16, 128), F32)
            for s in range(4):
                cls = jnp.broadcast_to(cb[block, s:s + 1, pl.ds(lane, 128)], (16, 128))
                val = jnp.broadcast_to(wb[block, s:s + 1, pl.ds(lane, 128)], (16, 128))
                acc = jnp.where(cls == rows, val, acc)
            wt[r:r + 16, pl.ds(wide, 128)] = acc.astype(BF16)
            result.append(total_acc[r // 16] + acc)
        return tuple(result)

    totals = lax.fori_loop(0, 28, spread, tuple(jnp.zeros((16, 128), F32) for _ in range(16)))

    row_id = lax.broadcasted_iota(jnp.int32, (16, 128), 0)
    lane_id = lax.broadcasted_iota(jnp.int32, (16, 128), 1)
    extra = []
    for i in range(16):
        column = jnp.broadcast_to(jnp.sum(totals[i], axis=1, keepdims=True), (16, 128))
        line = jnp.sum(jnp.where(row_id == lane_id, column, 0.0), axis=0, keepdims=True)
        high = line.astype(BF16).astype(F32)
        low = line - high
        extra.append(jnp.where(row_id == 12, high, jnp.where(row_id == 13, low, 0.0)))
    extra = jnp.concatenate(extra, axis=0)

    wide_row = lax.broadcasted_iota(jnp.int32, (256, 128), 0) % 16
    for h in (0, 1):
        for j in range(2):
            col = h * HALF + j * 256
            part_sum = jnp.dot(wt[...], sh[:, col:col + 256], preferred_element_type=F32)
            if j == 0:
                msg[h, :, 0:128] = jnp.where(wide_row < 12, part_sum[:, 0:128], extra).astype(BF16)
                msg[h, :, 128:256] = part_sum[:, 128:256].astype(BF16)
            else:
                msg[h, :, 256:512] = part_sum.astype(BF16)

    def msg_of(x_, y_, c_):
        blk = ((y_ // 2) * 4 + x_) * 2 + c_
        return msg.at[y_ % 2, pl.ds(pl.multiple_of(blk * 16, 16), 16), :]

    def final_copy(k):
        i = (me32 + k) % 32
        x_, y_, c_ = i // 8, (i // 2) % 4, i % 2
        return remote(msg_of(x_, y_, c_), fin.at[me32], fn_send.at[k], fn_recv.at[k], dev(x_, y_, c_, z))

    def send_final(k, _):
        final_copy(k).start()
        return 0

    lax.fori_loop(1, 32, send_final, 0)
    own_blk = ((y // 2) * 4 + x) * 2 + c
    fin[me32] = msg[y % 2, pl.ds(pl.multiple_of(own_blk * 16, 16), 16), :]

    def wait_final(k, _):
        final_copy(k).wait_recv()
        return 0

    lax.fori_loop(1, 32, wait_final, 0)

    def add(i, acc):
        return acc + fin[i].astype(F32)

    acc = lax.fori_loop(0, 32, add, jnp.zeros((16, HALF), F32))
    line = acc[12:13, 0:128] + acc[13:14, 0:128]
    den = jnp.sum(jnp.where(row_id == lane_id, jnp.broadcast_to(line, (16, 128)), 0.0), axis=1, keepdims=True) + 1.0
    out[...] = (acc / den)[0:12, :]

    for dc, dz in stage_offsets:
        stage_copy(dc, dz).wait_send()
    for dz in (1, 2, 3):
        for h in (0, 1):
            part_copy(dz, h).wait_send()
        cand_copy(dz).wait_send()
        weight_copy(dz).wait_send()
    for k in (1, 2, 3):
        first_send(k).wait_send()
        for a in range(4):
            second_send(a, k).wait_send()
    for a in range(4):
        for b_ in range(4):
            sib_copy(a, b_).wait_send()
    for p in range(3):
        rs_copy(p).wait_send()

    def left_final(k, _):
        final_copy(k).wait_send()
        return 0

    lax.fori_loop(1, 32, left_final, 0)


def on_device(particles, references, candidates, shifts, class_order):
    chosen = jnp.tile(candidates.T, (1, TRANS))
    chosen = jnp.pad(chosen, ((0, 4), (0, ROWS - TRANS * PART)), constant_values=-1)
    order = jnp.pad(class_order.reshape(16, 12), ((0, 0), (0, 4)), constant_values=-2).reshape(256, 1)
    moves = jnp.pad(shifts, ((0, 16 - TRANS), (0, 0)))
    dma = pltpu.SemaphoreType.DMA
    return pl.pallas_call(
        kernel,
        out_shape=jax.ShapeDtypeStruct((12, HALF), F32),
        in_specs=[
            pl.BlockSpec(memory_space=pl.ANY),
            pl.BlockSpec(memory_space=pl.ANY),
            pl.BlockSpec(memory_space=pltpu.VMEM),
            pl.BlockSpec(memory_space=pltpu.VMEM),
            pl.BlockSpec(memory_space=pltpu.VMEM),
        ],
        out_specs=pl.BlockSpec(memory_space=pltpu.VMEM),
        scratch_shapes=[
            pltpu.VMEM((8, 12, HALF), BF16),
            pltpu.VMEM((96, HALF), F32),
            pltpu.VMEM((2, REFS, HALF), BF16),
            pltpu.VMEM((4, 2, PART, HALF), BF16),
            pltpu.VMEM((4 * ROWS, 2 * HALF), BF16),
            pltpu.VMEM((4, 8, ROWS), jnp.int32),
            pltpu.VMEM((REFS, 128), F32),
            pltpu.VMEM((4, 32, ROWS), F32),
            pltpu.VMEM((3, 32, ROWS), F32),
            pltpu.VMEM((4, 8, ROWS), F32),
            pltpu.VMEM((256, 4 * ROWS), BF16),
            pltpu.VMEM((2, 256, HALF), BF16),
            pltpu.VMEM((32, 16, HALF), BF16),
            dma((8,)), dma((8,)), dma((8,)), dma((8,)), dma((4,)), dma((4,)),
            dma((16,)), dma((16,)), dma((16,)), dma((16,)), dma((3,)), dma((3,)),
            dma((3,)), dma((3,)), dma((32,)), dma((32,)),
        ],
        compiler_params=pltpu.CompilerParams(
            collective_id=0, has_side_effects=True, vmem_limit_bytes=56 * 2**20),
        name="estep",
    )(particles, references, chosen, moves, order)


def solution(mesh):
    return jax.shard_map(
        on_device,
        mesh=mesh,
        in_specs=(
            P(("blk", "grp"), None),
            P(("blk", "grp"), None),
            P(("blk", "grp"), None),
            P(),
            P(),
        ),
        out_specs=P("blk", "grp"),
        check_vma=False,
    )
```

```python
import math

import jax
import jax.numpy as jnp
from jax import lax
from jax.experimental import pallas as pl
from jax.experimental.pallas import tpu as pltpu
from jax.sharding import PartitionSpec as P

BOX = 128
ROT = 8
SCALE = 0.05
HALF = 512
PART = 96
TRANS = 9
ROWS = 896
CLS = 192
REFS = 1536
ORDER = (2, 1, 3, 0)
NT = (((1,), (1,)), ((), ()))
F32 = jnp.float32
BF16 = jnp.bfloat16


def pos_of(offset):
    return ORDER.index(offset % 4)


def kernel(
    parts, refs_in, cand_in, shifts, order_in, out,
    stage, stage32, refs, refs32, squares, hn, pb, table, sh, cand, cb, cs, order_row, order,
    gather_a, gather_b, e_out, e_in, wb, wt, totals, msg, fin,
    in_sem, st_send, st_recv, pt_send, pt_recv, cd_send, cd_recv,
    ag_send, ag_recv, sb_send, sb_recv, rs_send, rs_recv, ww_send, ww_recv, fn_send, fn_recv,
):
    b = lax.axis_index("blk")
    g = lax.axis_index("grp")
    c = b % 2
    x = (b // 2) % 4
    y = (b // 8) * 2 + g // 4
    z = g % 4

    def dev(x_, y_, c_, z_):
        return (((y_ // 2) * 4 + x_) * 2 + c_, (y_ % 2) * 4 + z_)

    def remote(src, dst, ssem, rsem, device):
        return pltpu.make_async_remote_copy(
            src_ref=src, dst_ref=dst, send_sem=ssem, recv_sem=rsem,
            device_id=device, device_id_type=pl.DeviceIdType.MESH)

    def zdev(delta):
        return dev(x, y, c, (z + delta) % 4)

    load_cand = pltpu.make_async_copy(cand_in, cand, in_sem.at[0])
    load_cand.start()
    load_order = pltpu.make_async_copy(order_in, order_row, in_sem.at[1])
    load_order.start()

    barrier = pltpu.get_barrier_semaphore()
    me32 = (x * 4 + y) * 2 + c

    def greet(k, _):
        i = (me32 + k) % 32
        pl.semaphore_signal(barrier, inc=1, device_id=dev(i // 8, (i // 2) % 4, i % 2, z),
                            device_id_type=pl.DeviceIdType.MESH)
        return 0

    lax.fori_loop(1, 32, greet, 0)
    for dz in (1, 2, 3):
        for dc in (0, 1):
            pl.semaphore_signal(barrier, inc=1, device_id=dev(x, y, (c + dc) % 2, (z + dz) % 4),
                                device_id_type=pl.DeviceIdType.MESH)
    load_cand.wait()
    own = cand[...]
    lanes = [jnp.concatenate([own[:, q * 16:q * 16 + 16]] * 8, axis=1) for q in range(6)]
    lanes.append(jnp.concatenate([own, jnp.full((4, 32), -1, jnp.int32)], axis=1))
    cb[3, 0:4, :] = jnp.concatenate(lanes, axis=1)
    pl.semaphore_wait(barrier, 37)

    def stage_copy(dc, dz):
        k = dc * 4 + dz
        c_ = (c + dc) % 2
        z_ = (z + dz) % 4
        cols = pl.ds(pl.multiple_of(c_ * 2048 + z_ * 512, 512), 512)
        return remote(refs_in.at[:, cols], stage.at[c * 4 + z], st_send.at[k], st_recv.at[k],
                      dev(x, y, c_, z_))

    stage_offsets = [(dc, dz) for dz in (2, 1, 3, 0) for dc in (0, 1) if dc or dz]
    for dc, dz in stage_offsets:
        stage_copy(dc, dz).start()
    own_cols = pl.ds(pl.multiple_of(c * 2048 + z * 512, 512), 512)
    own_stage = pltpu.make_async_copy(refs_in.at[:, own_cols], stage.at[c * 4 + z], st_recv.at[0])
    own_stage.start()

    def part_copy(dz, h):
        z_ = (z + dz) % 4
        cols = pl.ds(pl.multiple_of(h * 2048 + z_ * 512, 512), 512)
        p = pos_of(-dz)
        return remote(parts.at[:, cols], pb.at[p, h], pt_send.at[p * 2 + h], pt_recv.at[p * 2 + h], zdev(dz))

    def cand_copy(dz):
        p = pos_of(-dz)
        return remote(cb.at[3], cb.at[p], cd_send.at[p], cd_recv.at[p], zdev(dz))

    for dz in (1, 3, 2):
        cand_copy(dz).start()
    for dz in (1, 3, 2):
        for h in (0, 1):
            part_copy(dz, h).start()
    own_parts = []
    for h in (0, 1):
        cols = pl.ds(pl.multiple_of(h * 2048 + z * 512, 512), 512)
        own = pltpu.make_async_copy(parts.at[:, cols], pb.at[3, h], pt_recv.at[6 + h])
        own.start()
        own_parts.append(own)

    for dc, dz in stage_offsets:
        stage_copy(dc, dz).wait_recv()
    own_stage.wait()
    for i in range(8):
        stage32[i * 12:(i + 1) * 12, :] = stage[i].astype(F32)

    def block_rows(x_, y_):
        return pl.ds(pl.multiple_of((x_ * 4 + y_) * 96, 96), 96)

    refs[c, block_rows(x, y), :] = stage32[...].astype(BF16)

    def at(a, b_):
        dx = a * (1 - c) + b_ * c
        dy = b_ * (1 - c) + a * c
        return (x + dx) % 4, (y + dy) % 4

    def ref_block(a, b_):
        x_, y_ = at(a, b_)
        return refs.at[c, block_rows(x_, y_), :]

    def first_send(k):
        x_, y_ = at(k, 0)
        block = ref_block(0, 0)
        return remote(block, block, ag_send.at[k], ag_recv.at[((-k) % 4) * 4], dev(x_, y_, c, z))

    def second_send(a, k):
        x_, y_ = at(0, k)
        block = ref_block(a, 0)
        return remote(block, block, ag_send.at[3 + a * 3 + k], ag_recv.at[a * 4 + (-k) % 4], dev(x_, y_, c, z))

    def recv_block(a, b_):
        block = ref_block(a, b_)
        remote(block, block, ag_send.at[0], ag_recv.at[a * 4 + b_], dev(x, y, 1 - c, z)).wait_recv()

    def sib_copy(a, b_):
        block = ref_block(a, b_)
        return remote(block, block, sb_send.at[a * 4 + b_], sb_recv.at[a * 4 + b_], dev(x, y, 1 - c, z))

    for k in (2, 1, 3):
        first_send(k).start()
    for k in (2, 1, 3):
        second_send(0, k).start()
    sib_copy(0, 0).start()

    def shift_tables():
        index = lax.broadcasted_iota(jnp.int32, (16, HALF), 1) + z * HALF
        row = lax.broadcasted_iota(jnp.int32, (16, HALF), 0)
        turns = jnp.zeros((16, HALF), jnp.int32)
        for t in range(TRANS):
            line = shifts[0, t] * (index % (BOX // 2)) + shifts[1, t] * (index // (BOX // 2))
            turns = jnp.where(row == t, line, turns)
        angle = (turns & (BOX - 1)).astype(F32) * (2.0 * math.pi / BOX)
        table[0] = jnp.cos(angle)
        table[1] = jnp.sin(angle)

    def shift_block(p):
        base = p * ROWS
        sh[base + TRANS * PART:base + ROWS, :] = jnp.zeros((ROWS - TRANS * PART, 2 * HALF), BF16)

        def group(q, _):
            rows = pl.ds(pl.multiple_of(q * 16, 16), 16)
            re = pb[p, 0, rows, :].astype(F32)
            im = pb[p, 1, rows, :].astype(F32)
            for t in range(TRANS):
                co = table[0, t:t + 1, :]
                si = table[1, t:t + 1, :]
                row = base + q * 128 + t * 16 if t < 8 else base + 768 + q * 16
                dst = pl.ds(pl.multiple_of(row, 16), 16)
                sh[dst, 0:HALF] = (re * co - im * si).astype(BF16)
                sh[dst, HALF:2 * HALF] = (re * si + im * co).astype(BF16)
            return 0

        lax.fori_loop(0, 6, group, 0)

    def widen(h, x_, y_):
        for core in (0, 1):
            src = pl.ds(pl.multiple_of((x_ * 4 + y_) * 96 + core * 48, 48), 48)
            dst = pl.ds(((((y_ // 2) * 4 + x_) * 2 + core) * 2 + y_ % 2) * 6, 6)
            acc = jnp.zeros((48, 128), F32)
            for j in range(HALF // 128):
                v = refs[h, src, j * 128:(j + 1) * 128].astype(F32)
                refs32[h, dst, :, j * 128:(j + 1) * 128] = v.reshape(6, ROT, 128)
                acc = acc + v * v
            squares[h, dst] = acc.reshape(6, ROT, 128)

    shift_tables()
    for a in (1, 3, 2):
        recv_block(a, 0)
        for k in (2, 1, 3):
            second_send(a, k).start()
        sib_copy(a, 0).start()
    for copy in own_parts:
        copy.wait()
    shift_block(3)
    for a in range(4):
        widen(c, *at(a, 0))
    for b_ in (1, 3, 2):
        recv_block(0, b_)
        sib_copy(0, b_).start()
        widen(c, *at(0, b_))

    load_order.wait()
    row_id = lax.broadcasted_iota(jnp.int32, (16, 128), 0)
    lane_id = lax.broadcasted_iota(jnp.int32, (16, 128), 1)
    first = jnp.broadcast_to(order_row[:, 0:128], (16, 128)).astype(F32)
    rest_order = jnp.concatenate([order_row[:, 128:CLS], jnp.full((1, 256 - CLS), -1, jnp.int32)], axis=1)
    second = jnp.broadcast_to(rest_order, (16, 128)).astype(F32)
    for i in range(16):
        here = jnp.where(lane_id == i * 12 + row_id, first, 0.0)
        here = here + jnp.where(lane_id + 128 == i * 12 + row_id, second, 0.0)
        column = jnp.broadcast_to(jnp.sum(here, axis=1, keepdims=True), (16, 128))
        order[i * 16:i * 16 + 16, :] = jnp.where(row_id < 12, column, -2.0)

    for dz in (1, 3, 2):
        for h in (0, 1):
            part_copy(dz, h).wait_recv()
        cand_copy(dz).wait_recv()
        shift_block(pos_of(-dz))
        for b_ in (1, 3, 2):
            recv_block(dz, b_)
            sib_copy(dz, b_).start()
            widen(c, *at(dz, b_))
    for p in range(4):
        pltpu.make_async_copy(cb.at[p, :, pl.ds(768, 128)], cs.at[p], in_sem.at[2 + p]).start()
    for a in range(4):
        for b_ in range(4):
            sib_copy(a, b_).wait_recv()
    for p in range(4):
        pltpu.make_async_copy(cb.at[p, :, pl.ds(768, 128)], cs.at[p], in_sem.at[2 + p]).wait()

    def widen_rest(i, _):
        widen(1 - c, i // 4, i % 4)
        return 0

    lax.fori_loop(0, 16, widen_rest, 0)

    def norms(i, _):
        some = pl.ds(i * 12, 12)
        acc = squares[0, some] + squares[1, some]
        hn[some] = jnp.broadcast_to(0.5 * jnp.sum(acc, axis=2, keepdims=True), (12, ROT, 128))
        return 0

    lax.fori_loop(0, 16, norms, 0)

    def rs_copy(p):
        return remote(e_out.at[p], e_in.at[p], rs_send.at[p], rs_recv.at[p], zdev(ORDER[p]))

    def gather(dst, n):
        p, q = n // 6, n % 6
        for i in range(16):
            for s in (0, 2):
                first = cs[p, s, q * 16 + i]
                second = cs[p, s + 1, q * 16 + i]
                row = i * 32 + s * 8
                for h in (0, 1):
                    both = jnp.concatenate([refs32[h, first], refs32[h, second]], axis=0)
                    dst[row:row + 16, h * HALF:(h + 1) * HALF] = both.astype(BF16)

    tile_lane = lax.broadcasted_iota(jnp.int32, (8, 128), 1)

    def score(src, n):
        p, q = n // 6, n % 6
        lane = pl.multiple_of(q * 128, 128)
        base = p * ROWS
        moved = jnp.concatenate(
            [sh[pl.ds(pl.multiple_of(base + q * 128, 128), 128), :],
             sh[pl.ds(pl.multiple_of(base + 768, 128), 128), :]], axis=0)
        raw = lax.dot_general(src[...], moved, NT, preferred_element_type=F32)
        main = [jnp.zeros((8, 128), F32) for _ in range(4)]
        last = [e_out[p, s * 8:s * 8 + 8, 768:896] for s in range(4)]
        for i in range(16):
            in_main = (tile_lane & 15) == i
            in_last = tile_lane == q * 16 + i
            for s in range(4):
                row = i * 32 + s * 8
                norm = hn[cs[p, s, q * 16 + i]]
                main[s] = jnp.where(in_main, raw[row:row + 8, 0:128] - norm, main[s])
                last[s] = jnp.where(in_last, raw[row:row + 8, 128:256] - norm, last[s])
        for s in range(4):
            e_out[p, s * 8:s * 8 + 8, pl.ds(lane, 128)] = main[s]
            e_out[p, s * 8:s * 8 + 8, 768:896] = last[s]

    for p in range(4):
        e_out[p, :, 768:896] = jnp.zeros((32, 128), F32)
    gather(gather_a, 0)

    def scores(m, _):
        gather(gather_b, 2 * m + 1)
        score(gather_a, 2 * m)
        gather(gather_a, jnp.minimum(2 * m + 2, 23))
        score(gather_b, 2 * m + 1)
        for p in range(3):
            @pl.when(m == 3 * p + 2)
            def _():
                rs_copy(p).start()
        return 0

    lax.fori_loop(0, 12, scores, 0)

    for p in range(3):
        rs_copy(p).wait_recv()
    low = -1e30
    lane1 = lax.broadcasted_iota(jnp.int32, (8, 128), 1)
    row1 = lax.broadcasted_iota(jnp.int32, (8, 128), 0)

    def fold(rows, op, fill):
        wide = jnp.concatenate(rows[0:6] + [rows[5], rows[5]], axis=0)
        for step in (64, 32, 16):
            wide = op(wide, pltpu.roll(wide, step, 1))
        shifted = [rows[6]] + [pltpu.roll(rows[6], 128 - 16 * q, 1) for q in range(1, 6)]
        rest = jnp.concatenate(shifted + [shifted[5], shifted[5]], axis=0)
        rest = jnp.where(lane1 < 16, rest, fill)
        for step in (16, 32, 64):
            rest = op(rest, pltpu.roll(rest, step, 1))
        wide = op(wide, rest)
        final = jnp.sum(jnp.where((lane1 >> 4) == row1, wide, 0.0), axis=0, keepdims=True)
        return [wide[q:q + 1, :] for q in range(6)] + [final]

    logits = []
    for l in range(7):
        cols = slice(l * 128, l * 128 + 128)
        logits.append(SCALE * (e_out[3, :, cols] + e_in[0, :, cols] + e_in[1, :, cols] + e_in[2, :, cols]))
    top = fold([jnp.max(v, axis=0, keepdims=True) for v in logits], jnp.maximum, low)
    expo = [jnp.exp(v - t) for v, t in zip(logits, top)]
    total = fold([jnp.sum(v, axis=0, keepdims=True) for v in expo], jnp.add, 0.0)
    for l in range(7):
        rows = [jnp.sum(expo[l][s * 8:s * 8 + 8, :], axis=0, keepdims=True) for s in range(4)]
        weight = jnp.concatenate(rows + rows, axis=0) / total[l]
        if l == 6:
            weight = jnp.where(lane1 < PART, weight, 0.0)
        wb[3, :, l * 128:l * 128 + 128] = weight

    def weight_copy(dz):
        p = pos_of(-dz)
        return remote(wb.at[3], wb.at[p], ww_send.at[p], ww_recv.at[p], zdev(dz))

    for dz in (2, 1, 3):
        weight_copy(dz).start()
    def spread(p, first):
        for l in range(7):
            cols = slice(l * 128, l * 128 + 128)
            cls = [jnp.broadcast_to(cb[p, s:s + 1, cols], (8, 128)).astype(F32) for s in range(4)]
            val = [jnp.broadcast_to(wb[p, s:s + 1, cols], (8, 128)) for s in range(4)]
            for r in range(0, 256, 16):
                both = []
                for half in (r, r + 8):
                    rows = order[half:half + 8, :]
                    acc = jnp.zeros((8, 128), F32)
                    for s in range(4):
                        acc = jnp.where(cls[s] == rows, val[s], acc)
                    if first and l == 0:
                        totals[half:half + 8, :] = acc
                    else:
                        totals[half:half + 8, :] += acc
                    both.append(acc)
                wt[r:r + 16, p * ROWS + l * 128:p * ROWS + l * 128 + 128] = jnp.concatenate(both, axis=0).astype(BF16)

    spread(3, True)
    for dz in (1, 3, 2):
        weight_copy(dz).wait_recv()
        spread(pos_of(-dz), False)

    extra = []
    for i in range(16):
        column = jnp.broadcast_to(jnp.sum(totals[i * 16:i * 16 + 16, :], axis=1, keepdims=True), (16, 128))
        line = jnp.sum(jnp.where(row_id == lane_id, column, 0.0), axis=0, keepdims=True)
        high = line.astype(BF16).astype(F32)
        low = line - high
        extra.append(jnp.where(row_id == 12, high, jnp.where(row_id == 13, low, 0.0)))
    extra = jnp.concatenate(extra, axis=0)

    wide_row = lax.broadcasted_iota(jnp.int32, (256, 128), 0) % 16

    def msg_of(x_, y_, c_):
        blk = ((y_ // 2) * 4 + x_) * 2 + c_
        return msg.at[y_ % 2, pl.ds(pl.multiple_of(blk * 16, 16), 16), :]

    def final_copy(i):
        x_, y_, c_ = i // 8, (i // 2) % 4, i % 2
        return remote(msg_of(x_, y_, c_), fin.at[me32], fn_send.at[i], fn_recv.at[me32], dev(x_, y_, c_, z))

    def send_final(h, j):
        i = (((x + j // 4) % 4) * 4 + ((y // 2 + j // 2) % 2) * 2 + h) * 2 + (c + j) % 2

        @pl.when(i != me32)
        def _():
            final_copy(i).start()

        return 0

    for h in (0, 1):
        for j in range(2):
            col = h * HALF + j * 256
            part_sum = jnp.dot(wt[...], sh[:, col:col + 256], preferred_element_type=F32)
            if j == 0:
                msg[h, :, 0:128] = jnp.where(wide_row < 12, part_sum[:, 0:128], extra).astype(BF16)
                msg[h, :, 128:256] = part_sum[:, 128:256].astype(BF16)
            else:
                msg[h, :, 256:512] = part_sum.astype(BF16)
        lax.fori_loop(0, 16, lambda j, _: send_final(h, j), 0)

    fin[me32] = msg[y % 2, pl.ds(pl.multiple_of((((y // 2) * 4 + x) * 2 + c) * 16, 16), 16), :]

    def wait_final(i, _):
        @pl.when(i != me32)
        def _():
            remote(fin.at[i], fin.at[i], fn_send.at[i], fn_recv.at[i], dev(x, y, 1 - c, z)).wait_recv()

        return 0

    lax.fori_loop(0, 32, wait_final, 0)

    def add(i, acc):
        return acc + fin[i].astype(F32)

    acc = lax.fori_loop(0, 32, add, jnp.zeros((16, HALF), F32))
    line = acc[12:13, 0:128] + acc[13:14, 0:128]
    den = jnp.sum(jnp.where(row_id == lane_id, jnp.broadcast_to(line, (16, 128)), 0.0), axis=1, keepdims=True) + 1.0
    out[...] = (acc / den)[0:12, :]

    for dc, dz in stage_offsets:
        stage_copy(dc, dz).wait_send()
    for dz in (1, 2, 3):
        for h in (0, 1):
            part_copy(dz, h).wait_send()
        cand_copy(dz).wait_send()
        weight_copy(dz).wait_send()
    for k in (1, 2, 3):
        first_send(k).wait_send()
        for a in range(4):
            second_send(a, k).wait_send()
    for a in range(4):
        for b_ in range(4):
            sib_copy(a, b_).wait_send()
    for p in range(3):
        rs_copy(p).wait_send()

    def left_final(i, _):
        @pl.when(i != me32)
        def _():
            final_copy(i).wait_send()

        return 0

    lax.fori_loop(0, 32, left_final, 0)


def on_device(particles, references, candidates, shifts, class_order):
    dma = pltpu.SemaphoreType.DMA
    return pl.pallas_call(
        kernel,
        out_shape=jax.ShapeDtypeStruct((12, HALF), F32),
        in_specs=[
            pl.BlockSpec(memory_space=pl.ANY),
            pl.BlockSpec(memory_space=pl.ANY),
            pl.BlockSpec(memory_space=pl.ANY),
            pl.BlockSpec(memory_space=pltpu.SMEM),
            pl.BlockSpec(memory_space=pl.ANY),
        ],
        out_specs=pl.BlockSpec(memory_space=pltpu.VMEM),
        scratch_shapes=[
            pltpu.VMEM((8, 12, HALF), BF16),
            pltpu.VMEM((96, HALF), F32),
            pltpu.VMEM((2, REFS, HALF), BF16),
            pltpu.VMEM((2, CLS, ROT, HALF), F32),
            pltpu.VMEM((2, CLS, ROT, 128), F32),
            pltpu.VMEM((CLS, ROT, 128), F32),
            pltpu.VMEM((4, 2, PART, HALF), BF16),
            pltpu.VMEM((2, 16, HALF), F32),
            pltpu.VMEM((4 * ROWS, 2 * HALF), BF16),
            pltpu.VMEM((4, PART), jnp.int32),
            pltpu.VMEM((4, 8, ROWS), jnp.int32),
            pltpu.SMEM((4, 8, 128), jnp.int32),
            pltpu.VMEM((1, CLS), jnp.int32),
            pltpu.VMEM((256, 128), F32),
            pltpu.VMEM((512, 2 * HALF), BF16),
            pltpu.VMEM((512, 2 * HALF), BF16),
            pltpu.VMEM((4, 32, ROWS), F32),
            pltpu.VMEM((3, 32, ROWS), F32),
            pltpu.VMEM((4, 8, ROWS), F32),
            pltpu.VMEM((256, 4 * ROWS), BF16),
            pltpu.VMEM((256, 128), F32),
            pltpu.VMEM((2, 256, HALF), BF16),
            pltpu.VMEM((32, 16, HALF), BF16),
            dma((6,)),
            dma((8,)), dma((8,)), dma((8,)), dma((8,)), dma((4,)), dma((4,)),
            dma((16,)), dma((16,)), dma((16,)), dma((16,)), dma((3,)), dma((3,)),
            dma((3,)), dma((3,)), dma((32,)), dma((32,)),
        ],
        compiler_params=pltpu.CompilerParams(
            collective_id=0, has_side_effects=True, vmem_limit_bytes=56 * 2**20),
        name="estep",
    )(particles, references, candidates.T, shifts.T, class_order.reshape(1, CLS))


def solution(mesh):
    return jax.shard_map(
        on_device,
        mesh=mesh,
        in_specs=(
            P(("blk", "grp"), None),
            P(("blk", "grp"), None),
            P(("blk", "grp"), None),
            P(),
            P(),
        ),
        out_specs=P("blk", "grp"),
        check_vma=False,
    )
```

```python
import math

import jax
import jax.numpy as jnp
from jax import lax
from jax.experimental import pallas as pl
from jax.experimental.pallas import tpu as pltpu
from jax.sharding import PartitionSpec as P

BOX = 128
ROT = 8
SCALE = 0.05
HALF = 512
PART = 96
TRANS = 9
ROWS = 896
CLS = 192
REFS = 1536
ORDER = (2, 1, 3, 0)
NT = (((1,), (1,)), ((), ()))
F32 = jnp.float32
BF16 = jnp.bfloat16


def pos_of(offset):
    return ORDER.index(offset % 4)


def kernel(
    parts, refs_in, cand_in, shifts, order_in, out,
    refs_own, parts_own, stage, stage32, refs, refs32, squares, hn, pb, table, sh, cand, cb, cs, order_row, order,
    gather_a, gather_b, e_out, e_in, wb, wt, totals, msg, fin,
    in_sem, st_send, st_recv, pt_send, pt_recv, cd_send, cd_recv,
    ag_send, ag_recv, sb_send, sb_recv, rs_send, rs_recv, ww_send, ww_recv, fn_send, fn_recv,
):
    b = lax.axis_index("blk")
    g = lax.axis_index("grp")
    c = b % 2
    x = (b // 2) % 4
    y = (b // 8) * 2 + g // 4
    z = g % 4

    def dev(x_, y_, c_, z_):
        return (((y_ // 2) * 4 + x_) * 2 + c_, (y_ % 2) * 4 + z_)

    def remote(src, dst, ssem, rsem, device):
        return pltpu.make_async_remote_copy(
            src_ref=src, dst_ref=dst, send_sem=ssem, recv_sem=rsem,
            device_id=device, device_id_type=pl.DeviceIdType.MESH)

    def zdev(delta):
        return dev(x, y, c, (z + delta) % 4)

    def shift_tables():
        index = lax.broadcasted_iota(jnp.int32, (16, HALF), 1) + z * HALF
        row = lax.broadcasted_iota(jnp.int32, (16, HALF), 0)
        turns = jnp.zeros((16, HALF), jnp.int32)
        for t in range(TRANS):
            line = shifts[0, t] * (index % (BOX // 2)) + shifts[1, t] * (index // (BOX // 2))
            turns = jnp.where(row == t, line, turns)
        angle = (turns & (BOX - 1)).astype(F32) * (2.0 * math.pi / BOX)
        table[0] = jnp.cos(angle)
        table[1] = jnp.sin(angle)

    def shift_block(p):
        base = p * ROWS
        sh[base + TRANS * PART:base + ROWS, :] = jnp.zeros((ROWS - TRANS * PART, 2 * HALF), BF16)

        def group(q, _):
            rows = pl.ds(pl.multiple_of(q * 16, 16), 16)
            if p == 3:
                re = parts_own[rows, pl.ds(pl.multiple_of(z * HALF, HALF), HALF)].astype(F32)
                im = parts_own[rows, pl.ds(pl.multiple_of(2048 + z * HALF, HALF), HALF)].astype(F32)
            else:
                re = pb[p, 0, rows, :].astype(F32)
                im = pb[p, 1, rows, :].astype(F32)
            for t in range(TRANS):
                co = table[0, t:t + 1, :]
                si = table[1, t:t + 1, :]
                row = base + q * 128 + t * 16 if t < 8 else base + 768 + q * 16
                dst = pl.ds(pl.multiple_of(row, 16), 16)
                sh[dst, 0:HALF] = (re * co - im * si).astype(BF16)
                sh[dst, HALF:2 * HALF] = (re * si + im * co).astype(BF16)
            return 0

        lax.fori_loop(0, 6, group, 0)

    load_cand = pltpu.make_async_copy(cand_in, cand, in_sem.at[0])
    load_cand.start()
    load_order = pltpu.make_async_copy(order_in, order_row, in_sem.at[1])
    load_order.start()

    load_refs = pltpu.make_async_copy(refs_in, refs_own, in_sem.at[6])
    load_refs.start()
    load_parts = pltpu.make_async_copy(parts, parts_own, in_sem.at[7])
    load_parts.start()

    barrier = pltpu.get_barrier_semaphore()
    me32 = (x * 4 + y) * 2 + c

    def greet(device):
        pl.semaphore_signal(barrier, inc=1, device_id=device, device_id_type=pl.DeviceIdType.MESH)

    for k in (1, 2, 3):
        greet(dev((x + k) % 4, y, c, z))
        greet(dev(x, (y + k) % 4, c, z))
    for dz in (1, 2, 3):
        for dc in (0, 1):
            greet(dev(x, y, (c + dc) % 2, (z + dz) % 4))
    greet(dev(x, y, 1 - c, z))
    load_cand.wait()
    own = cand[...]
    lanes = [jnp.concatenate([own[:, q * 16:q * 16 + 16]] * 8, axis=1) for q in range(6)]
    lanes.append(jnp.concatenate([own, jnp.full((4, 32), -1, jnp.int32)], axis=1))
    cb[3, 0:4, :] = jnp.concatenate(lanes, axis=1)
    load_refs.wait()
    load_parts.wait()
    pl.semaphore_wait(barrier, 13)

    def stage_copy(dc, dz):
        k = dc * 4 + dz
        c_ = (c + dc) % 2
        z_ = (z + dz) % 4
        cols = pl.ds(pl.multiple_of(c_ * 2048 + z_ * 512, 512), 512)
        return remote(refs_own.at[:, cols], stage.at[c * 4 + z], st_send.at[k], st_recv.at[k],
                      dev(x, y, c_, z_))

    stage_offsets = [(dc, dz) for dz in (2, 1, 3, 0) for dc in (0, 1) if dc or dz]
    for dc, dz in stage_offsets:
        stage_copy(dc, dz).start()
    own_cols = pl.ds(pl.multiple_of(c * 2048 + z * 512, 512), 512)
    stage[c * 4 + z] = refs_own[:, own_cols]

    def part_copy(dz, h):
        z_ = (z + dz) % 4
        cols = pl.ds(pl.multiple_of(h * 2048 + z_ * 512, 512), 512)
        p = pos_of(-dz)
        return remote(parts_own.at[:, cols], pb.at[p, h], pt_send.at[p * 2 + h], pt_recv.at[p * 2 + h], zdev(dz))

    def cand_copy(dz):
        p = pos_of(-dz)
        return remote(cb.at[3], cb.at[p], cd_send.at[p], cd_recv.at[p], zdev(dz))

    for dz in (1, 3, 2):
        cand_copy(dz).start()
    for dz in (1, 3, 2):
        for h in (0, 1):
            part_copy(dz, h).start()

    shift_tables()
    shift_block(3)

    for dc, dz in stage_offsets:
        stage_copy(dc, dz).wait_recv()
    for i in range(8):
        stage32[i * 12:(i + 1) * 12, :] = stage[i].astype(F32)

    def block_rows(x_, y_):
        return pl.ds(pl.multiple_of((x_ * 4 + y_) * 96, 96), 96)

    refs[c, block_rows(x, y), :] = stage32[...].astype(BF16)

    def at(a, b_):
        dx = a * (1 - c) + b_ * c
        dy = b_ * (1 - c) + a * c
        return (x + dx) % 4, (y + dy) % 4

    def ref_block(a, b_):
        x_, y_ = at(a, b_)
        return refs.at[c, block_rows(x_, y_), :]

    def first_send(k):
        x_, y_ = at(k, 0)
        block = ref_block(0, 0)
        return remote(block, block, ag_send.at[k], ag_recv.at[((-k) % 4) * 4], dev(x_, y_, c, z))

    def second_send(a, k):
        x_, y_ = at(0, k)
        block = ref_block(a, 0)
        return remote(block, block, ag_send.at[3 + a * 3 + k], ag_recv.at[a * 4 + (-k) % 4], dev(x_, y_, c, z))

    def recv_block(a, b_):
        block = ref_block(a, b_)
        remote(block, block, ag_send.at[0], ag_recv.at[a * 4 + b_], dev(x, y, 1 - c, z)).wait_recv()

    def sib_copy(a, b_):
        block = ref_block(a, b_)
        return remote(block, block, sb_send.at[a * 4 + b_], sb_recv.at[a * 4 + b_], dev(x, y, 1 - c, z))

    for k in (2, 1, 3):
        first_send(k).start()
    sib_copy(0, 0).start()
    for k in (2, 1, 3):
        first_send(k).wait_send()
    for k in (2, 1, 3):
        second_send(0, k).start()

    def widen(h, x_, y_):
        for core in (0, 1):
            src = pl.ds(pl.multiple_of((x_ * 4 + y_) * 96 + core * 48, 48), 48)
            dst = pl.ds(((((y_ // 2) * 4 + x_) * 2 + core) * 2 + y_ % 2) * 6, 6)
            acc = jnp.zeros((48, 128), F32)
            for j in range(HALF // 128):
                v = refs[h, src, j * 128:(j + 1) * 128].astype(F32)
                refs32[h, dst, :, j * 128:(j + 1) * 128] = v.reshape(6, ROT, 128)
                acc = acc + v * v
            squares[h, dst] = acc.reshape(6, ROT, 128)

    for a in (1, 3, 2):
        recv_block(a, 0)
        for k in (2, 1, 3):
            second_send(a, k).start()
        sib_copy(a, 0).start()
    for a in range(4):
        widen(c, *at(a, 0))
    for b_ in (1, 3, 2):
        recv_block(0, b_)
        sib_copy(0, b_).start()
        widen(c, *at(0, b_))

    load_order.wait()
    row_id = lax.broadcasted_iota(jnp.int32, (16, 128), 0)
    lane_id = lax.broadcasted_iota(jnp.int32, (16, 128), 1)
    first = jnp.broadcast_to(order_row[:, 0:128], (16, 128)).astype(F32)
    rest_order = jnp.concatenate([order_row[:, 128:CLS], jnp.full((1, 256 - CLS), -1, jnp.int32)], axis=1)
    second = jnp.broadcast_to(rest_order, (16, 128)).astype(F32)
    for i in range(16):
        here = jnp.where(lane_id == i * 12 + row_id, first, 0.0)
        here = here + jnp.where(lane_id + 128 == i * 12 + row_id, second, 0.0)
        column = jnp.broadcast_to(jnp.sum(here, axis=1, keepdims=True), (16, 128))
        order[i * 16:i * 16 + 16, :] = jnp.where(row_id < 12, column, -2.0)

    for dz in (1, 3, 2):
        for h in (0, 1):
            part_copy(dz, h).wait_recv()
        cand_copy(dz).wait_recv()
        shift_block(pos_of(-dz))
        for b_ in (1, 3, 2):
            recv_block(dz, b_)
            sib_copy(dz, b_).start()
            widen(c, *at(dz, b_))
    for p in range(4):
        pltpu.make_async_copy(cb.at[p, :, pl.ds(768, 128)], cs.at[p], in_sem.at[2 + p]).start()
    for a in range(4):
        for b_ in range(4):
            sib_copy(a, b_).wait_recv()
    for p in range(4):
        pltpu.make_async_copy(cb.at[p, :, pl.ds(768, 128)], cs.at[p], in_sem.at[2 + p]).wait()

    def widen_rest(i, _):
        widen(1 - c, i // 4, i % 4)
        return 0

    lax.fori_loop(0, 16, widen_rest, 0)

    def norms(i, _):
        some = pl.ds(i * 12, 12)
        acc = squares[0, some] + squares[1, some]
        hn[some] = jnp.broadcast_to(0.5 * jnp.sum(acc, axis=2, keepdims=True), (12, ROT, 128))
        return 0

    lax.fori_loop(0, 16, norms, 0)

    def rs_copy(p):
        return remote(e_out.at[p], e_in.at[p], rs_send.at[p], rs_recv.at[p], zdev(ORDER[p]))

    def gather(dst, p, q):
        for i in range(16):
            for s in (0, 2):
                first = cs[p, s, q * 16 + i]
                second = cs[p, s + 1, q * 16 + i]
                row = i * 32 + s * 8
                for h in (0, 1):
                    both = jnp.concatenate([refs32[h, first], refs32[h, second]], axis=0)
                    dst[row:row + 16, h * HALF:(h + 1) * HALF] = both.astype(BF16)

    tile_lane = lax.broadcasted_iota(jnp.int32, (8, 128), 1)

    def score(src, p, q, last):
        base = p * ROWS
        moved = jnp.concatenate(
            [sh[pl.ds(pl.multiple_of(base + q * 128, 128), 128), :],
             sh[pl.ds(pl.multiple_of(base + 768, 128), 128), :]], axis=0)
        raw = lax.dot_general(src[...], moved, NT, preferred_element_type=F32)
        main = [jnp.zeros((8, 128), F32) for _ in range(4)]
        for i in range(16):
            in_main = (tile_lane & 15) == i
            in_last = tile_lane == q * 16 + i
            for s in range(4):
                row = i * 32 + s * 8
                norm = hn[cs[p, s, q * 16 + i]]
                main[s] = jnp.where(in_main, raw[row:row + 8, 0:128] - norm, main[s])
                last[s] = jnp.where(in_last, raw[row:row + 8, 128:256] - norm, last[s])
        for s in range(4):
            e_out[p, s * 8:s * 8 + 8, q * 128:q * 128 + 128] = main[s]
        return last

    gather(gather_a, 0, 0)

    def scores(p, _):
        last = [jnp.zeros((8, 128), F32) for _ in range(4)]
        for q in range(6):
            here, ahead = (gather_a, gather_b) if q % 2 == 0 else (gather_b, gather_a)
            if q < 5:
                gather(ahead, p, q + 1)
            else:
                gather(ahead, jnp.minimum(p + 1, 3), 0)
            last = score(here, p, q, last)
        for s in range(4):
            e_out[p, s * 8:s * 8 + 8, 768:896] = last[s]
        for k in range(3):
            @pl.when(p == k)
            def _():
                rs_copy(k).start()
        return 0

    lax.fori_loop(0, 4, scores, 0)

    for p in range(3):
        rs_copy(p).wait_recv()
    low = -1e30
    lane1 = lax.broadcasted_iota(jnp.int32, (8, 128), 1)
    row1 = lax.broadcasted_iota(jnp.int32, (8, 128), 0)

    def fold(rows, op, fill):
        wide = jnp.concatenate(rows[0:6] + [rows[5], rows[5]], axis=0)
        for step in (64, 32, 16):
            wide = op(wide, pltpu.roll(wide, step, 1))
        shifted = [rows[6]] + [pltpu.roll(rows[6], 128 - 16 * q, 1) for q in range(1, 6)]
        rest = jnp.concatenate(shifted + [shifted[5], shifted[5]], axis=0)
        rest = jnp.where(lane1 < 16, rest, fill)
        for step in (16, 32, 64):
            rest = op(rest, pltpu.roll(rest, step, 1))
        wide = op(wide, rest)
        final = jnp.sum(jnp.where((lane1 >> 4) == row1, wide, 0.0), axis=0, keepdims=True)
        return [wide[q:q + 1, :] for q in range(6)] + [final]

    logits = []
    for l in range(7):
        cols = slice(l * 128, l * 128 + 128)
        logits.append(SCALE * (e_out[3, :, cols] + e_in[0, :, cols] + e_in[1, :, cols] + e_in[2, :, cols]))
    top = fold([jnp.max(v, axis=0, keepdims=True) for v in logits], jnp.maximum, low)
    expo = [jnp.exp(v - t) for v, t in zip(logits, top)]
    total = fold([jnp.sum(v, axis=0, keepdims=True) for v in expo], jnp.add, 0.0)
    for l in range(7):
        rows = [jnp.sum(expo[l][s * 8:s * 8 + 8, :], axis=0, keepdims=True) for s in range(4)]
        weight = jnp.concatenate(rows + rows, axis=0) / total[l]
        if l == 6:
            weight = jnp.where(lane1 < PART, weight, 0.0)
        wb[3, :, l * 128:l * 128 + 128] = weight

    def weight_copy(dz):
        p = pos_of(-dz)
        return remote(wb.at[3], wb.at[p], ww_send.at[p], ww_recv.at[p], zdev(dz))

    for dz in (2, 1, 3):
        weight_copy(dz).start()
    def spread(p, first):
        for l in range(7):
            cols = slice(l * 128, l * 128 + 128)
            cls = [jnp.broadcast_to(cb[p, s:s + 1, cols], (8, 128)).astype(F32) for s in range(4)]
            val = [jnp.broadcast_to(wb[p, s:s + 1, cols], (8, 128)) for s in range(4)]
            for r in range(0, 256, 16):
                both = []
                for half in (r, r + 8):
                    rows = order[half:half + 8, :]
                    acc = jnp.zeros((8, 128), F32)
                    for s in range(4):
                        acc = jnp.where(cls[s] == rows, val[s], acc)
                    if first and l == 0:
                        totals[half:half + 8, :] = acc
                    else:
                        totals[half:half + 8, :] += acc
                    both.append(acc)
                wt[r:r + 16, p * ROWS + l * 128:p * ROWS + l * 128 + 128] = jnp.concatenate(both, axis=0).astype(BF16)

    spread(3, True)
    for dz in (1, 3, 2):
        weight_copy(dz).wait_recv()
        spread(pos_of(-dz), False)

    extra = []
    for i in range(16):
        column = jnp.broadcast_to(jnp.sum(totals[i * 16:i * 16 + 16, :], axis=1, keepdims=True), (16, 128))
        line = jnp.sum(jnp.where(row_id == lane_id, column, 0.0), axis=0, keepdims=True)
        high = line.astype(BF16).astype(F32)
        low = line - high
        extra.append(jnp.where(row_id == 12, high, jnp.where(row_id == 13, low, 0.0)))
    extra = jnp.concatenate(extra, axis=0)

    wide_row = lax.broadcasted_iota(jnp.int32, (256, 128), 0) % 16

    def msg_of(x_, y_, c_):
        blk = ((y_ // 2) * 4 + x_) * 2 + c_
        return msg.at[y_ % 2, pl.ds(pl.multiple_of(blk * 16, 16), 16), :]

    def final_copy(i):
        x_, y_, c_ = i // 8, (i // 2) % 4, i % 2
        return remote(msg_of(x_, y_, c_), fin.at[me32], fn_send.at[i], fn_recv.at[me32], dev(x_, y_, c_, z))

    def send_final(h, j):
        i = (((x + j // 4) % 4) * 4 + ((y // 2 + j // 2) % 2) * 2 + h) * 2 + (c + j) % 2

        @pl.when(i != me32)
        def _():
            final_copy(i).start()

        return 0

    for h in (0, 1):
        for j in range(2):
            col = h * HALF + j * 256
            part_sum = jnp.dot(wt[...], sh[:, col:col + 256], preferred_element_type=F32)
            if j == 0:
                msg[h, :, 0:128] = jnp.where(wide_row < 12, part_sum[:, 0:128], extra).astype(BF16)
                msg[h, :, 128:256] = part_sum[:, 128:256].astype(BF16)
            else:
                msg[h, :, 256:512] = part_sum.astype(BF16)
        lax.fori_loop(0, 16, lambda j, _: send_final(h, j), 0)

    fin[me32] = msg[y % 2, pl.ds(pl.multiple_of((((y // 2) * 4 + x) * 2 + c) * 16, 16), 16), :]

    def wait_final(i, _):
        @pl.when(i != me32)
        def _():
            remote(fin.at[i], fin.at[i], fn_send.at[i], fn_recv.at[i], dev(x, y, 1 - c, z)).wait_recv()

        return 0

    lax.fori_loop(0, 32, wait_final, 0)

    def add(i, acc):
        return acc + fin[i].astype(F32)

    acc = lax.fori_loop(0, 32, add, jnp.zeros((16, HALF), F32))
    line = acc[12:13, 0:128] + acc[13:14, 0:128]
    den = jnp.sum(jnp.where(row_id == lane_id, jnp.broadcast_to(line, (16, 128)), 0.0), axis=1, keepdims=True) + 1.0
    out[...] = (acc / den)[0:12, :]

    for dc, dz in stage_offsets:
        stage_copy(dc, dz).wait_send()
    for dz in (1, 2, 3):
        for h in (0, 1):
            part_copy(dz, h).wait_send()
        cand_copy(dz).wait_send()
        weight_copy(dz).wait_send()
    for k in (1, 2, 3):
        for a in range(4):
            second_send(a, k).wait_send()
    for a in range(4):
        for b_ in range(4):
            sib_copy(a, b_).wait_send()
    for p in range(3):
        rs_copy(p).wait_send()

    def left_final(i, _):
        @pl.when(i != me32)
        def _():
            final_copy(i).wait_send()

        return 0

    lax.fori_loop(0, 32, left_final, 0)


def on_device(particles, references, candidates, shifts, class_order):
    dma = pltpu.SemaphoreType.DMA
    return pl.pallas_call(
        kernel,
        out_shape=jax.ShapeDtypeStruct((12, HALF), F32),
        in_specs=[
            pl.BlockSpec(memory_space=pl.ANY),
            pl.BlockSpec(memory_space=pl.ANY),
            pl.BlockSpec(memory_space=pl.ANY),
            pl.BlockSpec(memory_space=pltpu.SMEM),
            pl.BlockSpec(memory_space=pl.ANY),
        ],
        out_specs=pl.BlockSpec(memory_space=pltpu.VMEM),
        scratch_shapes=[
            pltpu.VMEM((12, 4096), BF16),
            pltpu.VMEM((PART, 4096), BF16),
            pltpu.VMEM((8, 12, HALF), BF16),
            pltpu.VMEM((96, HALF), F32),
            pltpu.VMEM((2, REFS, HALF), BF16),
            pltpu.VMEM((2, CLS, ROT, HALF), F32),
            pltpu.VMEM((2, CLS, ROT, 128), F32),
            pltpu.VMEM((CLS, ROT, 128), F32),
            pltpu.VMEM((3, 2, PART, HALF), BF16),
            pltpu.VMEM((2, 16, HALF), F32),
            pltpu.VMEM((4 * ROWS, 2 * HALF), BF16),
            pltpu.VMEM((4, PART), jnp.int32),
            pltpu.VMEM((4, 8, ROWS), jnp.int32),
            pltpu.SMEM((4, 8, 128), jnp.int32),
            pltpu.VMEM((1, CLS), jnp.int32),
            pltpu.VMEM((256, 128), F32),
            pltpu.VMEM((512, 2 * HALF), BF16),
            pltpu.VMEM((512, 2 * HALF), BF16),
            pltpu.VMEM((4, 32, ROWS), F32),
            pltpu.VMEM((3, 32, ROWS), F32),
            pltpu.VMEM((4, 8, ROWS), F32),
            pltpu.VMEM((256, 4 * ROWS), BF16),
            pltpu.VMEM((256, 128), F32),
            pltpu.VMEM((2, 256, HALF), BF16),
            pltpu.VMEM((32, 16, HALF), BF16),
            dma((8,)),
            dma((8,)), dma((8,)), dma((8,)), dma((8,)), dma((4,)), dma((4,)),
            dma((16,)), dma((16,)), dma((16,)), dma((16,)), dma((3,)), dma((3,)),
            dma((3,)), dma((3,)), dma((32,)), dma((32,)),
        ],
        compiler_params=pltpu.CompilerParams(
            collective_id=0, has_side_effects=True, vmem_limit_bytes=56 * 2**20),
        name="estep",
    )(particles, references, candidates.T, shifts.T, class_order.reshape(1, CLS))


def solution(mesh):
    return jax.shard_map(
        on_device,
        mesh=mesh,
        in_specs=(
            P(("blk", "grp"), None),
            P(("blk", "grp"), None),
            P(("blk", "grp"), None),
            P(),
            P(),
        ),
        out_specs=P("blk", "grp"),
        check_vma=False,
    )
```

```python
import math

import jax
import jax.numpy as jnp
from jax import lax
from jax.experimental import pallas as pl
from jax.experimental.pallas import tpu as pltpu
from jax.sharding import PartitionSpec as P

BOX = 128
ROT = 8
SCALE = 0.05
HALF = 512
PART = 96
TRANS = 9
ROWS = 896
CLS = 192
REFS = 1536
ORDER = (2, 1, 3, 0)
NT = (((1,), (1,)), ((), ()))
F32 = jnp.float32
BF16 = jnp.bfloat16


def pos_of(offset):
    return ORDER.index(offset % 4)


def kernel(
    parts, refs_in, cand_in, shifts, order_in, out,
    refs_own, parts_own, stage, stage32, refs, refs32, squares, hn, pb, table, sh, cand, cb, cs, order_row, order,
    gather_a, gather_b, e_out, e_in, wb, wt, totals, sums, pair_out, pair_in, msg, fin,
    in_sem, st_send, st_recv, pt_send, pt_recv, cd_send, cd_recv,
    ag_send, ag_recv, sb_send, sb_recv, rs_send, rs_recv, ww_send, ww_recv, pr_send, pr_recv, fn_send, fn_recv,
):
    b = lax.axis_index("blk")
    g = lax.axis_index("grp")
    c = b % 2
    x = (b // 2) % 4
    y = (b // 8) * 2 + g // 4
    z = g % 4

    def dev(x_, y_, c_, z_):
        return (((y_ // 2) * 4 + x_) * 2 + c_, (y_ % 2) * 4 + z_)

    def remote(src, dst, ssem, rsem, device):
        return pltpu.make_async_remote_copy(
            src_ref=src, dst_ref=dst, send_sem=ssem, recv_sem=rsem,
            device_id=device, device_id_type=pl.DeviceIdType.MESH)

    def zdev(delta):
        return dev(x, y, c, (z + delta) % 4)

    def shift_tables():
        index = lax.broadcasted_iota(jnp.int32, (16, HALF), 1) + z * HALF
        row = lax.broadcasted_iota(jnp.int32, (16, HALF), 0)
        turns = jnp.zeros((16, HALF), jnp.int32)
        for t in range(TRANS):
            line = shifts[0, t] * (index % (BOX // 2)) + shifts[1, t] * (index // (BOX // 2))
            turns = jnp.where(row == t, line, turns)
        angle = (turns & (BOX - 1)).astype(F32) * (2.0 * math.pi / BOX)
        table[0] = jnp.cos(angle)
        table[1] = jnp.sin(angle)

    def shift_block(p):
        base = p * ROWS
        sh[base + TRANS * PART:base + ROWS, :] = jnp.zeros((ROWS - TRANS * PART, 2 * HALF), BF16)

        def group(q, _):
            rows = pl.ds(pl.multiple_of(q * 16, 16), 16)
            if p == 3:
                re = parts_own[rows, pl.ds(pl.multiple_of(z * HALF, HALF), HALF)].astype(F32)
                im = parts_own[rows, pl.ds(pl.multiple_of(2048 + z * HALF, HALF), HALF)].astype(F32)
            else:
                re = pb[p, 0, rows, :].astype(F32)
                im = pb[p, 1, rows, :].astype(F32)
            for t in range(TRANS):
                co = table[0, t:t + 1, :]
                si = table[1, t:t + 1, :]
                row = base + q * 128 + t * 16 if t < 8 else base + 768 + q * 16
                dst = pl.ds(pl.multiple_of(row, 16), 16)
                sh[dst, 0:HALF] = (re * co - im * si).astype(BF16)
                sh[dst, HALF:2 * HALF] = (re * si + im * co).astype(BF16)
            return 0

        lax.fori_loop(0, 6, group, 0)

    barrier = pltpu.get_barrier_semaphore()

    def greet(device):
        pl.semaphore_signal(barrier, inc=1, device_id=device, device_id_type=pl.DeviceIdType.MESH)

    for k in (1, 2, 3):
        greet(dev((x + k) % 4, y, c, z))
        greet(dev(x, (y + k) % 4, c, z))
    for dz in (1, 2, 3):
        for dc in (0, 1):
            greet(dev(x, y, (c + dc) % 2, (z + dz) % 4))
    greet(dev(x, y, 1 - c, z))
    load_cand = pltpu.make_async_copy(cand_in, cand, in_sem.at[0])
    load_cand.start()
    load_order = pltpu.make_async_copy(order_in, order_row, in_sem.at[1])
    load_order.start()

    load_refs = pltpu.make_async_copy(refs_in, refs_own, in_sem.at[6])
    load_refs.start()
    load_parts = pltpu.make_async_copy(parts, parts_own, in_sem.at[7])
    load_parts.start()

    load_refs.wait()
    pl.semaphore_wait(barrier, 13)

    def stage_copy(dc, dz):
        k = dc * 4 + dz
        c_ = (c + dc) % 2
        z_ = (z + dz) % 4
        cols = pl.ds(pl.multiple_of(c_ * 2048 + z_ * 512, 512), 512)
        return remote(refs_own.at[:, cols], stage.at[c * 4 + z], st_send.at[k], st_recv.at[k],
                      dev(x, y, c_, z_))

    stage_offsets = [(dc, dz) for dz in (2, 1, 3, 0) for dc in (0, 1) if dc or dz]
    for dc, dz in stage_offsets:
        stage_copy(dc, dz).start()
    own_cols = pl.ds(pl.multiple_of(c * 2048 + z * 512, 512), 512)
    stage[c * 4 + z] = refs_own[:, own_cols]

    def part_copy(dz, h):
        z_ = (z + dz) % 4
        cols = pl.ds(pl.multiple_of(h * 2048 + z_ * 512, 512), 512)
        p = pos_of(-dz)
        return remote(parts_own.at[:, cols], pb.at[p, h], pt_send.at[p * 2 + h], pt_recv.at[p * 2 + h], zdev(dz))

    def cand_copy(dz):
        p = pos_of(-dz)
        return remote(cb.at[3], cb.at[p], cd_send.at[p], cd_recv.at[p], zdev(dz))

    load_parts.wait()
    for dz in (1, 3, 2):
        for h in (0, 1):
            part_copy(dz, h).start()
    load_cand.wait()
    own = cand[...]
    lanes = [jnp.concatenate([own[:, q * 16:q * 16 + 16]] * 8, axis=1) for q in range(6)]
    lanes.append(jnp.concatenate([own, jnp.full((4, 32), -1, jnp.int32)], axis=1))
    cb[3, 0:4, :] = jnp.concatenate(lanes, axis=1)
    for dz in (1, 3, 2):
        cand_copy(dz).start()

    for dc, dz in stage_offsets:
        stage_copy(dc, dz).wait_recv()
    for i in range(8):
        stage32[i * 12:(i + 1) * 12, :] = stage[i].astype(F32)

    def block_rows(x_, y_):
        return pl.ds(pl.multiple_of((x_ * 4 + y_) * 96, 96), 96)

    refs[c, block_rows(x, y), :] = stage32[...].astype(BF16)

    def at(a, b_):
        dx = a * (1 - c) + b_ * c
        dy = b_ * (1 - c) + a * c
        return (x + dx) % 4, (y + dy) % 4

    def ref_block(a, b_):
        x_, y_ = at(a, b_)
        return refs.at[c, block_rows(x_, y_), :]

    def first_send(k):
        x_, y_ = at(k, 0)
        block = ref_block(0, 0)
        return remote(block, block, ag_send.at[k], ag_recv.at[((-k) % 4) * 4], dev(x_, y_, c, z))

    def second_send(a, k):
        x_, y_ = at(0, k)
        block = ref_block(a, 0)
        return remote(block, block, ag_send.at[3 + a * 3 + k], ag_recv.at[a * 4 + (-k) % 4], dev(x_, y_, c, z))

    def recv_block(a, b_):
        block = ref_block(a, b_)
        remote(block, block, ag_send.at[0], ag_recv.at[a * 4 + b_], dev(x, y, 1 - c, z)).wait_recv()

    def sib_copy(a, b_):
        block = ref_block(a, b_)
        return remote(block, block, sb_send.at[a * 4 + b_], sb_recv.at[a * 4 + b_], dev(x, y, 1 - c, z))

    for k in (2, 1, 3):
        first_send(k).start()
    sib_copy(0, 0).start()
    shift_tables()
    shift_block(3)
    for k in (2, 1, 3):
        first_send(k).wait_send()
    for k in (2, 1, 3):
        second_send(0, k).start()

    def widen(h, x_, y_):
        for core in (0, 1):
            src = pl.ds(pl.multiple_of((x_ * 4 + y_) * 96 + core * 48, 48), 48)
            dst = pl.ds(((((y_ // 2) * 4 + x_) * 2 + core) * 2 + y_ % 2) * 6, 6)
            acc = jnp.zeros((48, 128), F32)
            for j in range(HALF // 128):
                v = refs[h, src, j * 128:(j + 1) * 128].astype(F32)
                refs32[h, dst, :, j * 128:(j + 1) * 128] = v.reshape(6, ROT, 128)
                acc = acc + v * v
            squares[h, dst] = acc.reshape(6, ROT, 128)

    for a in (1, 3, 2):
        recv_block(a, 0)
        for k in (2, 1, 3):
            second_send(a, k).start()
        sib_copy(a, 0).start()
    for a in range(4):
        widen(c, *at(a, 0))
    for b_ in (1, 3, 2):
        recv_block(0, b_)
        sib_copy(0, b_).start()
        widen(c, *at(0, b_))

    load_order.wait()
    row_id = lax.broadcasted_iota(jnp.int32, (16, 128), 0)
    lane_id = lax.broadcasted_iota(jnp.int32, (16, 128), 1)
    first = jnp.broadcast_to(order_row[:, 0:128], (16, 128)).astype(F32)
    rest_order = jnp.concatenate([order_row[:, 128:CLS], jnp.full((1, 256 - CLS), -1, jnp.int32)], axis=1)
    second = jnp.broadcast_to(rest_order, (16, 128)).astype(F32)
    for i in range(16):
        start = ((i % 8) * 2 + i // 8) * 12
        here = jnp.where(lane_id == start + row_id, first, 0.0)
        here = here + jnp.where(lane_id + 128 == start + row_id, second, 0.0)
        column = jnp.broadcast_to(jnp.sum(here, axis=1, keepdims=True), (16, 128))
        order[i * 16:i * 16 + 16, :] = jnp.where(row_id < 12, column, -2.0)

    for dz in (1, 3, 2):
        for h in (0, 1):
            part_copy(dz, h).wait_recv()
        cand_copy(dz).wait_recv()
        shift_block(pos_of(-dz))
        for b_ in (1, 3, 2):
            recv_block(dz, b_)
            sib_copy(dz, b_).start()
            widen(c, *at(dz, b_))
    for p in range(4):
        pltpu.make_async_copy(cb.at[p, :, pl.ds(768, 128)], cs.at[p], in_sem.at[2 + p]).start()
    for a in range(4):
        for b_ in range(4):
            sib_copy(a, b_).wait_recv()
    for p in range(4):
        pltpu.make_async_copy(cb.at[p, :, pl.ds(768, 128)], cs.at[p], in_sem.at[2 + p]).wait()

    def widen_rest(i, _):
        widen(1 - c, i // 4, i % 4)
        return 0

    lax.fori_loop(0, 16, widen_rest, 0)

    def norms(i, _):
        some = pl.ds(i * 12, 12)
        acc = squares[0, some] + squares[1, some]
        hn[some] = jnp.broadcast_to(0.5 * jnp.sum(acc, axis=2, keepdims=True), (12, ROT, 128))
        return 0

    lax.fori_loop(0, 16, norms, 0)

    def rs_copy(p):
        return remote(e_out.at[p], e_in.at[p], rs_send.at[p], rs_recv.at[p], zdev(ORDER[p]))

    def gather(dst, p, q):
        for i in range(16):
            for s in (0, 2):
                first = cs[p, s, q * 16 + i]
                second = cs[p, s + 1, q * 16 + i]
                row = i * 32 + s * 8
                for h in (0, 1):
                    both = jnp.concatenate([refs32[h, first], refs32[h, second]], axis=0)
                    dst[row:row + 16, h * HALF:(h + 1) * HALF] = both.astype(BF16)

    tile_lane = lax.broadcasted_iota(jnp.int32, (8, 128), 1)

    def score(src, p, q, last):
        base = p * ROWS
        moved = jnp.concatenate(
            [sh[pl.ds(pl.multiple_of(base + q * 128, 128), 128), :],
             sh[pl.ds(pl.multiple_of(base + 768, 128), 128), :]], axis=0)
        raw = lax.dot_general(src[...], moved, NT, preferred_element_type=F32)
        main = [jnp.zeros((8, 128), F32) for _ in range(4)]
        for i in range(16):
            in_main = (tile_lane & 15) == i
            in_last = tile_lane == q * 16 + i
            for s in range(4):
                row = i * 32 + s * 8
                norm = hn[cs[p, s, q * 16 + i]]
                main[s] = jnp.where(in_main, raw[row:row + 8, 0:128] - norm, main[s])
                last[s] = jnp.where(in_last, raw[row:row + 8, 128:256] - norm, last[s])
        for s in range(4):
            e_out[p, s * 8:s * 8 + 8, q * 128:q * 128 + 128] = main[s]
        return last

    gather(gather_a, 0, 0)

    def scores(p, _):
        last = [jnp.zeros((8, 128), F32) for _ in range(4)]
        for q in range(6):
            here, ahead = (gather_a, gather_b) if q % 2 == 0 else (gather_b, gather_a)
            if q < 5:
                gather(ahead, p, q + 1)
            else:
                gather(ahead, jnp.minimum(p + 1, 3), 0)
            last = score(here, p, q, last)
        for s in range(4):
            e_out[p, s * 8:s * 8 + 8, 768:896] = last[s]
        for k in range(3):
            @pl.when(p == k)
            def _():
                rs_copy(k).start()
        return 0

    lax.fori_loop(0, 4, scores, 0)

    for p in range(3):
        rs_copy(p).wait_recv()
    low = -1e30
    lane1 = lax.broadcasted_iota(jnp.int32, (8, 128), 1)
    row1 = lax.broadcasted_iota(jnp.int32, (8, 128), 0)

    def fold(rows, op, fill):
        wide = jnp.concatenate(rows[0:6] + [rows[5], rows[5]], axis=0)
        for step in (64, 32, 16):
            wide = op(wide, pltpu.roll(wide, step, 1))
        shifted = [rows[6]] + [pltpu.roll(rows[6], 128 - 16 * q, 1) for q in range(1, 6)]
        rest = jnp.concatenate(shifted + [shifted[5], shifted[5]], axis=0)
        rest = jnp.where(lane1 < 16, rest, fill)
        for step in (16, 32, 64):
            rest = op(rest, pltpu.roll(rest, step, 1))
        wide = op(wide, rest)
        final = jnp.sum(jnp.where((lane1 >> 4) == row1, wide, 0.0), axis=0, keepdims=True)
        return [wide[q:q + 1, :] for q in range(6)] + [final]

    logits = []
    for l in range(7):
        cols = slice(l * 128, l * 128 + 128)
        logits.append(SCALE * (e_out[3, :, cols] + e_in[0, :, cols] + e_in[1, :, cols] + e_in[2, :, cols]))
    top = fold([jnp.max(v, axis=0, keepdims=True) for v in logits], jnp.maximum, low)
    expo = [jnp.exp(v - t) for v, t in zip(logits, top)]
    total = fold([jnp.sum(v, axis=0, keepdims=True) for v in expo], jnp.add, 0.0)
    for l in range(7):
        rows = [jnp.sum(expo[l][s * 8:s * 8 + 8, :], axis=0, keepdims=True) for s in range(4)]
        weight = jnp.concatenate(rows + rows, axis=0) / total[l]
        if l == 6:
            weight = jnp.where(lane1 < PART, weight, 0.0)
        wb[3, :, l * 128:l * 128 + 128] = weight

    def weight_copy(dz):
        p = pos_of(-dz)
        return remote(wb.at[3], wb.at[p], ww_send.at[p], ww_recv.at[p], zdev(dz))

    for dz in (2, 1, 3):
        weight_copy(dz).start()
    def spread(p, first):
        for l in range(7):
            cols = slice(l * 128, l * 128 + 128)
            cls = [jnp.broadcast_to(cb[p, s:s + 1, cols], (8, 128)).astype(F32) for s in range(4)]
            val = [jnp.broadcast_to(wb[p, s:s + 1, cols], (8, 128)) for s in range(4)]
            for r in range(0, 256, 16):
                both = []
                for half in (r, r + 8):
                    rows = order[half:half + 8, :]
                    acc = jnp.zeros((8, 128), F32)
                    for s in range(4):
                        acc = jnp.where(cls[s] == rows, val[s], acc)
                    if first and l == 0:
                        totals[half:half + 8, :] = acc
                    else:
                        totals[half:half + 8, :] += acc
                    both.append(acc)
                wt[r:r + 16, p * ROWS + l * 128:p * ROWS + l * 128 + 128] = jnp.concatenate(both, axis=0).astype(BF16)

    spread(3, True)
    for dz in (1, 3, 2):
        weight_copy(dz).wait_recv()
        spread(pos_of(-dz), False)

    extra = []
    for i in range(16):
        column = jnp.broadcast_to(jnp.sum(totals[i * 16:i * 16 + 16, :], axis=1, keepdims=True), (16, 128))
        line = jnp.sum(jnp.where(row_id == lane_id, column, 0.0), axis=0, keepdims=True)
        high = line.astype(BF16).astype(F32)
        low = line - high
        extra.append(jnp.where(row_id == 12, high, jnp.where(row_id == 13, low, 0.0)))
    extra = jnp.concatenate(extra, axis=0)

    wide_row = lax.broadcasted_iota(jnp.int32, (256, 128), 0) % 16
    mine = pl.ds(pl.multiple_of(c * 128, 128), 128)
    theirs = pl.ds(pl.multiple_of((1 - c) * 128, 128), 128)

    def pair_copy(h):
        return remote(pair_out.at[h], pair_in.at[h], pr_send.at[h], pr_recv.at[h], dev(x, y, 1 - c, z))

    for h in (0, 1):
        for j in range(2):
            col = h * HALF + j * 256
            part_sum = jnp.dot(wt[...], sh[:, col:col + 256], preferred_element_type=F32)
            if j == 0:
                sums[h, :, 0:128] = jnp.where(wide_row < 12, part_sum[:, 0:128], extra)
                sums[h, :, 128:256] = part_sum[:, 128:256]
            else:
                sums[h, :, 256:512] = part_sum
        pair_out[h] = sums[h, theirs, :].astype(BF16)
        pair_copy(h).start()

    me16 = x * 4 + y

    def final_copy(i):
        x_, y_ = i // 4, i % 4
        rows = pl.ds(pl.multiple_of(((y_ // 2) * 4 + x_) * 16, 16), 16)
        return remote(msg.at[y_ % 2, rows, :], fin.at[me16], fn_send.at[i], fn_recv.at[me16], dev(x_, y_, c, z))

    def send_final(h, j):
        i = ((x + j // 2) % 4) * 4 + ((y // 2 + j) % 2) * 2 + h

        @pl.when(i != me16)
        def _():
            final_copy(i).start()

        return 0

    for h in (0, 1):
        pair_copy(h).wait_recv()
        both = sums[h, mine, :] + pair_in[h].astype(F32)
        msg[h, :, 128:HALF] = both[:, 128:HALF].astype(BF16)
        first = both[:, 0:128]
        whole = first + pltpu.roll(first, 127, 0)
        high = whole.astype(BF16).astype(F32)
        low = pltpu.roll(whole - high, 1, 0)
        first = jnp.where(wide_row[0:128] == 12, high, jnp.where(wide_row[0:128] == 13, low, first))
        msg[h, :, 0:128] = first.astype(BF16)
        lax.fori_loop(0, 8, lambda j, _: send_final(h, j), 0)

    own_row = pl.ds(pl.multiple_of(((y // 2) * 4 + x) * 16, 16), 16)
    fin[me16] = msg[y % 2, own_row, :]

    def wait_final(i, _):
        @pl.when(i != me16)
        def _():
            remote(fin.at[i], fin.at[i], fn_send.at[i], fn_recv.at[i], dev(x, y, 1 - c, z)).wait_recv()

        return 0

    lax.fori_loop(0, 16, wait_final, 0)

    acc = fin[0].astype(F32)
    for i in range(1, 16):
        acc = acc + fin[i].astype(F32)
    line = acc[12:13, 0:128] + acc[13:14, 0:128]
    den = jnp.sum(jnp.where(row_id == lane_id, jnp.broadcast_to(line, (16, 128)), 0.0), axis=1, keepdims=True) + 1.0
    out[...] = (acc / den)[0:12, :]

    for dc, dz in stage_offsets:
        stage_copy(dc, dz).wait_send()
    for dz in (1, 2, 3):
        for h in (0, 1):
            part_copy(dz, h).wait_send()
        cand_copy(dz).wait_send()
        weight_copy(dz).wait_send()
    for k in (1, 2, 3):
        for a in range(4):
            second_send(a, k).wait_send()
    for a in range(4):
        for b_ in range(4):
            sib_copy(a, b_).wait_send()
    for p in range(3):
        rs_copy(p).wait_send()

    def left_final(i, _):
        @pl.when(i != me16)
        def _():
            final_copy(i).wait_send()

        return 0

    lax.fori_loop(0, 16, left_final, 0)
    for h in (0, 1):
        pair_copy(h).wait_send()


def on_device(particles, references, candidates, shifts, class_order):
    dma = pltpu.SemaphoreType.DMA
    return pl.pallas_call(
        kernel,
        out_shape=jax.ShapeDtypeStruct((12, HALF), F32),
        in_specs=[
            pl.BlockSpec(memory_space=pl.ANY),
            pl.BlockSpec(memory_space=pl.ANY),
            pl.BlockSpec(memory_space=pl.ANY),
            pl.BlockSpec(memory_space=pltpu.SMEM),
            pl.BlockSpec(memory_space=pl.ANY),
        ],
        out_specs=pl.BlockSpec(memory_space=pltpu.VMEM),
        scratch_shapes=[
            pltpu.VMEM((12, 4096), BF16),
            pltpu.VMEM((PART, 4096), BF16),
            pltpu.VMEM((8, 12, HALF), BF16),
            pltpu.VMEM((96, HALF), F32),
            pltpu.VMEM((2, REFS, HALF), BF16),
            pltpu.VMEM((2, CLS, ROT, HALF), F32),
            pltpu.VMEM((2, CLS, ROT, 128), F32),
            pltpu.VMEM((CLS, ROT, 128), F32),
            pltpu.VMEM((3, 2, PART, HALF), BF16),
            pltpu.VMEM((2, 16, HALF), F32),
            pltpu.VMEM((4 * ROWS, 2 * HALF), BF16),
            pltpu.VMEM((4, PART), jnp.int32),
            pltpu.VMEM((4, 8, ROWS), jnp.int32),
            pltpu.SMEM((4, 8, 128), jnp.int32),
            pltpu.VMEM((1, CLS), jnp.int32),
            pltpu.VMEM((256, 128), F32),
            pltpu.VMEM((512, 2 * HALF), BF16),
            pltpu.VMEM((512, 2 * HALF), BF16),
            pltpu.VMEM((4, 32, ROWS), F32),
            pltpu.VMEM((3, 32, ROWS), F32),
            pltpu.VMEM((4, 8, ROWS), F32),
            pltpu.VMEM((256, 4 * ROWS), BF16),
            pltpu.VMEM((256, 128), F32),
            pltpu.VMEM((2, 256, HALF), F32),
            pltpu.VMEM((2, 128, HALF), BF16),
            pltpu.VMEM((2, 128, HALF), BF16),
            pltpu.VMEM((2, 128, HALF), BF16),
            pltpu.VMEM((16, 16, HALF), BF16),
            dma((8,)),
            dma((8,)), dma((8,)), dma((8,)), dma((8,)), dma((4,)), dma((4,)),
            dma((16,)), dma((16,)), dma((16,)), dma((16,)), dma((3,)), dma((3,)),
            dma((3,)), dma((3,)), dma((2,)), dma((2,)), dma((16,)), dma((16,)),
        ],
        compiler_params=pltpu.CompilerParams(
            collective_id=0, has_side_effects=True, vmem_limit_bytes=56 * 2**20),
        name="estep",
    )(particles, references, candidates.T, shifts.T, class_order.reshape(1, CLS))


def solution(mesh):
    return jax.shard_map(
        on_device,
        mesh=mesh,
        in_specs=(
            P(("blk", "grp"), None),
            P(("blk", "grp"), None),
            P(("blk", "grp"), None),
            P(),
            P(),
        ),
        out_specs=P("blk", "grp"),
        check_vma=False,
    )
```

```python
import math

import jax
import jax.numpy as jnp
from jax import lax
from jax.experimental import pallas as pl
from jax.experimental.pallas import tpu as pltpu
from jax.sharding import PartitionSpec as P

BOX = 128
ROT = 8
SCALE = 0.05
HALF = 512
PART = 96
TRANS = 9
ROWS = 896
CLS = 192
REFS = 1536
ORDER = (2, 1, 3, 0)
NT = (((1,), (1,)), ((), ()))
F32 = jnp.float32
BF16 = jnp.bfloat16


def pos_of(offset):
    return ORDER.index(offset % 4)


def kernel(
    parts, refs_in, cand_in, shifts, order_in, out,
    refs_own, parts_own, stage, stage32, refs, refs32, squares, hn, pb, table, sh, cand, cb, cs, order_row, order,
    gather_a, gather_b, e_out, e_in, wb, wt, totals, sums, pair_out, pair_in, msg, fin,
    in_sem, st_send, st_recv, pt_send, pt_recv, cd_send, cd_recv,
    ag_send, ag_recv, sb_send, sb_recv, rs_send, rs_recv, ww_send, ww_recv, pr_send, pr_recv, fn_send, fn_recv,
):
    b = lax.axis_index("blk")
    g = lax.axis_index("grp")
    c = b % 2
    x = (b // 2) % 4
    y = (b // 8) * 2 + g // 4
    z = g % 4

    def dev(x_, y_, c_, z_):
        return (((y_ // 2) * 4 + x_) * 2 + c_, (y_ % 2) * 4 + z_)

    def remote(src, dst, ssem, rsem, device):
        return pltpu.make_async_remote_copy(
            src_ref=src, dst_ref=dst, send_sem=ssem, recv_sem=rsem,
            device_id=device, device_id_type=pl.DeviceIdType.MESH)

    def zdev(delta):
        return dev(x, y, c, (z + delta) % 4)

    def shift_tables():
        index = lax.broadcasted_iota(jnp.int32, (16, HALF), 1) + z * HALF
        row = lax.broadcasted_iota(jnp.int32, (16, HALF), 0)
        turns = jnp.zeros((16, HALF), jnp.int32)
        for t in range(TRANS):
            line = shifts[0, t] * (index % (BOX // 2)) + shifts[1, t] * (index // (BOX // 2))
            turns = jnp.where(row == t, line, turns)
        angle = (turns & (BOX - 1)).astype(F32) * (2.0 * math.pi / BOX)
        table[0] = jnp.cos(angle)
        table[1] = jnp.sin(angle)

    def shift_block(p):
        base = p * ROWS
        sh[base + TRANS * PART:base + ROWS, :] = jnp.zeros((ROWS - TRANS * PART, 2 * HALF), BF16)

        def group(q, _):
            rows = pl.ds(pl.multiple_of(q * 16, 16), 16)
            if p == 3:
                re = parts_own[rows, pl.ds(pl.multiple_of(z * HALF, HALF), HALF)].astype(F32)
                im = parts_own[rows, pl.ds(pl.multiple_of(2048 + z * HALF, HALF), HALF)].astype(F32)
            else:
                re = pb[p, 0, rows, :].astype(F32)
                im = pb[p, 1, rows, :].astype(F32)
            for t in range(TRANS):
                co = table[0, t:t + 1, :]
                si = table[1, t:t + 1, :]
                row = base + q * 128 + t * 16 if t < 8 else base + 768 + q * 16
                dst = pl.ds(pl.multiple_of(row, 16), 16)
                sh[dst, 0:HALF] = (re * co - im * si).astype(BF16)
                sh[dst, HALF:2 * HALF] = (re * si + im * co).astype(BF16)
            return 0

        lax.fori_loop(0, 6, group, 0)

    barrier = pltpu.get_barrier_semaphore()

    def greet(device):
        pl.semaphore_signal(barrier, inc=1, device_id=device, device_id_type=pl.DeviceIdType.MESH)

    for k in (1, 2, 3):
        greet(dev((x + k) % 4, y, c, z))
        greet(dev(x, (y + k) % 4, c, z))
    for dz in (1, 2, 3):
        for dc in (0, 1):
            greet(dev(x, y, (c + dc) % 2, (z + dz) % 4))
    greet(dev(x, y, 1 - c, z))
    load_cand = pltpu.make_async_copy(cand_in, cand, in_sem.at[0])
    load_cand.start()
    load_order = pltpu.make_async_copy(order_in, order_row, in_sem.at[1])
    load_order.start()

    load_refs = pltpu.make_async_copy(refs_in, refs_own, in_sem.at[6])
    load_refs.start()
    load_parts = pltpu.make_async_copy(parts, parts_own, in_sem.at[7])
    load_parts.start()

    load_refs.wait()
    pl.semaphore_wait(barrier, 13)

    def stage_copy(dc, dz):
        k = dc * 4 + dz
        c_ = (c + dc) % 2
        z_ = (z + dz) % 4
        cols = pl.ds(pl.multiple_of(c_ * 2048 + z_ * 512, 512), 512)
        return remote(refs_own.at[:, cols], stage.at[c * 4 + z], st_send.at[k], st_recv.at[k],
                      dev(x, y, c_, z_))

    stage_offsets = [(dc, dz) for dz in (2, 1, 3, 0) for dc in (0, 1) if dc or dz]
    for dc, dz in stage_offsets:
        stage_copy(dc, dz).start()
    own_cols = pl.ds(pl.multiple_of(c * 2048 + z * 512, 512), 512)
    stage[c * 4 + z] = refs_own[:, own_cols]

    def part_copy(dz, h):
        z_ = (z + dz) % 4
        cols = pl.ds(pl.multiple_of(h * 2048 + z_ * 512, 512), 512)
        p = pos_of(-dz)
        return remote(parts_own.at[:, cols], pb.at[p, h], pt_send.at[p * 2 + h], pt_recv.at[p * 2 + h], zdev(dz))

    def cand_copy(dz):
        p = pos_of(-dz)
        return remote(cb.at[3], cb.at[p], cd_send.at[p], cd_recv.at[p], zdev(dz))

    for dc, dz in stage_offsets:
        stage_copy(dc, dz).wait_recv()
    for i in range(8):
        stage32[i * 12:(i + 1) * 12, :] = stage[i].astype(F32)

    def block_rows(x_, y_):
        return pl.ds(pl.multiple_of((x_ * 4 + y_) * 96, 96), 96)

    refs[c, block_rows(x, y), :] = stage32[...].astype(BF16)

    def at(a, b_, core=None):
        core = c if core is None else core
        dx = a * (1 - core) + b_ * core
        dy = b_ * (1 - core) + a * core
        return (x + dx) % 4, (y + dy) % 4

    def ref_block(a, b_):
        x_, y_ = at(a, b_)
        return refs.at[c, block_rows(x_, y_), :]

    def first_send(k):
        x_, y_ = at(k, 0)
        block = ref_block(0, 0)
        return remote(block, block, ag_send.at[k], ag_recv.at[((-k) % 4) * 4], dev(x_, y_, c, z))

    def second_send(a, k):
        x_, y_ = at(0, k)
        block = ref_block(a, 0)
        return remote(block, block, ag_send.at[3 + a * 3 + k], ag_recv.at[a * 4 + (-k) % 4], dev(x_, y_, c, z))

    def recv_block(a, b_):
        block = ref_block(a, b_)
        remote(block, block, ag_send.at[0], ag_recv.at[a * 4 + b_], dev(x, y, 1 - c, z)).wait_recv()

    def sib_copy(a, b_):
        block = ref_block(a, b_)
        return remote(block, block, sb_send.at[a * 4 + b_], sb_recv.at[a * 4 + b_], dev(x, y, 1 - c, z))

    for k in (2, 1, 3):
        first_send(k).start()
    sib_copy(0, 0).start()
    load_parts.wait()
    for dz in (1, 3, 2):
        for h in (0, 1):
            part_copy(dz, h).start()
    load_cand.wait()
    own = cand[...]
    lanes = [jnp.concatenate([own[:, q * 16:q * 16 + 16]] * 8, axis=1) for q in range(6)]
    lanes.append(jnp.concatenate([own, jnp.full((4, 32), -1, jnp.int32)], axis=1))
    cb[3, 0:4, :] = jnp.concatenate(lanes, axis=1)
    for dz in (1, 3, 2):
        cand_copy(dz).start()

    shift_tables()
    shift_block(3)
    for k in (2, 1, 3):
        first_send(k).wait_send()
    for k in (2, 1, 3):
        second_send(0, k).start()

    def widen(h, x_, y_):
        for core in (0, 1):
            src = pl.ds(pl.multiple_of((x_ * 4 + y_) * 96 + core * 48, 48), 48)
            dst = pl.ds(((((y_ // 2) * 4 + x_) * 2 + core) * 2 + y_ % 2) * 6, 6)
            acc = jnp.zeros((48, 128), F32)
            for j in range(HALF // 128):
                v = refs[h, src, j * 128:(j + 1) * 128].astype(F32)
                refs32[h, dst, :, j * 128:(j + 1) * 128] = v.reshape(6, ROT, 128)
                acc = acc + v * v
            squares[h, dst] = acc.reshape(6, ROT, 128)

    for a in (1, 3, 2):
        recv_block(a, 0)
        for k in (2, 1, 3):
            second_send(a, k).start()
        sib_copy(a, 0).start()
    for a in range(4):
        widen(c, *at(a, 0))
    for b_ in (1, 3, 2):
        recv_block(0, b_)
        sib_copy(0, b_).start()
        widen(c, *at(0, b_))

    load_order.wait()
    row_id = lax.broadcasted_iota(jnp.int32, (16, 128), 0)
    lane_id = lax.broadcasted_iota(jnp.int32, (16, 128), 1)
    first = jnp.broadcast_to(order_row[:, 0:128], (16, 128)).astype(F32)
    rest_order = jnp.concatenate([order_row[:, 128:CLS], jnp.full((1, 256 - CLS), -1, jnp.int32)], axis=1)
    second = jnp.broadcast_to(rest_order, (16, 128)).astype(F32)
    for i in range(16):
        start = ((i % 8) * 2 + i // 8) * 12
        here = jnp.where(lane_id == start + row_id, first, 0.0)
        here = here + jnp.where(lane_id + 128 == start + row_id, second, 0.0)
        column = jnp.broadcast_to(jnp.sum(here, axis=1, keepdims=True), (16, 128))
        order[i * 16:i * 16 + 16, :] = jnp.where(row_id < 12, column, -2.0)

    for dz in (1, 3, 2):
        for h in (0, 1):
            part_copy(dz, h).wait_recv()
        cand_copy(dz).wait_recv()
        shift_block(pos_of(-dz))
        for b_ in (1, 3, 2):
            recv_block(dz, b_)
            sib_copy(dz, b_).start()
            widen(c, *at(dz, b_))
    for p in range(4):
        pltpu.make_async_copy(cb.at[p, :, pl.ds(768, 128)], cs.at[p], in_sem.at[2 + p]).start()
    arrivals = [(a, 0) for a in (0, 1, 3, 2)] + [(0, b_) for b_ in (1, 3, 2)]
    arrivals += [(a, b_) for a in (1, 3, 2) for b_ in (1, 3, 2)]
    for a, b_ in arrivals:
        sib_copy(a, b_).wait_recv()
        widen(1 - c, *at(a, b_, 1 - c))
    for p in range(4):
        pltpu.make_async_copy(cb.at[p, :, pl.ds(768, 128)], cs.at[p], in_sem.at[2 + p]).wait()

    def norms(i, _):
        some = pl.ds(i * 12, 12)
        acc = squares[0, some] + squares[1, some]
        hn[some] = jnp.broadcast_to(0.5 * jnp.sum(acc, axis=2, keepdims=True), (12, ROT, 128))
        return 0

    lax.fori_loop(0, 16, norms, 0)

    def rs_copy(p):
        return remote(e_out.at[p], e_in.at[p], rs_send.at[p], rs_recv.at[p], zdev(ORDER[p]))

    def gather(dst, p, q):
        for i in range(16):
            for s in (0, 2):
                first = cs[p, s, q * 16 + i]
                second = cs[p, s + 1, q * 16 + i]
                row = i * 32 + s * 8
                for h in (0, 1):
                    both = jnp.concatenate([refs32[h, first], refs32[h, second]], axis=0)
                    dst[row:row + 16, h * HALF:(h + 1) * HALF] = both.astype(BF16)

    tile_lane = lax.broadcasted_iota(jnp.int32, (8, 128), 1)

    def score(src, p, q, last):
        base = p * ROWS
        moved = jnp.concatenate(
            [sh[pl.ds(pl.multiple_of(base + q * 128, 128), 128), :],
             sh[pl.ds(pl.multiple_of(base + 768, 128), 128), :]], axis=0)
        raw = lax.dot_general(src[...], moved, NT, preferred_element_type=F32)
        main = [jnp.zeros((8, 128), F32) for _ in range(4)]
        for i in range(16):
            in_main = (tile_lane & 15) == i
            in_last = tile_lane == q * 16 + i
            for s in range(4):
                row = i * 32 + s * 8
                norm = hn[cs[p, s, q * 16 + i]]
                main[s] = jnp.where(in_main, raw[row:row + 8, 0:128] - norm, main[s])
                last[s] = jnp.where(in_last, raw[row:row + 8, 128:256] - norm, last[s])
        for s in range(4):
            e_out[p, s * 8:s * 8 + 8, q * 128:q * 128 + 128] = main[s]
        return last

    gather(gather_a, 0, 0)

    def scores(p, _):
        last = [jnp.zeros((8, 128), F32) for _ in range(4)]
        for q in range(6):
            here, ahead = (gather_a, gather_b) if q % 2 == 0 else (gather_b, gather_a)
            if q < 5:
                gather(ahead, p, q + 1)
            else:
                gather(ahead, jnp.minimum(p + 1, 3), 0)
            last = score(here, p, q, last)
        for s in range(4):
            e_out[p, s * 8:s * 8 + 8, 768:896] = last[s]
        for k in range(3):
            @pl.when(p == k)
            def _():
                rs_copy(k).start()
        return 0

    lax.fori_loop(0, 4, scores, 0)

    for p in range(3):
        rs_copy(p).wait_recv()
    low = -1e30
    lane1 = lax.broadcasted_iota(jnp.int32, (8, 128), 1)
    row1 = lax.broadcasted_iota(jnp.int32, (8, 128), 0)

    def fold(rows, op, fill):
        wide = jnp.concatenate(rows[0:6] + [rows[5], rows[5]], axis=0)
        for step in (64, 32, 16):
            wide = op(wide, pltpu.roll(wide, step, 1))
        shifted = [rows[6]] + [pltpu.roll(rows[6], 128 - 16 * q, 1) for q in range(1, 6)]
        rest = jnp.concatenate(shifted + [shifted[5], shifted[5]], axis=0)
        rest = jnp.where(lane1 < 16, rest, fill)
        for step in (16, 32, 64):
            rest = op(rest, pltpu.roll(rest, step, 1))
        wide = op(wide, rest)
        final = jnp.sum(jnp.where((lane1 >> 4) == row1, wide, 0.0), axis=0, keepdims=True)
        return [wide[q:q + 1, :] for q in range(6)] + [final]

    logits = []
    for l in range(7):
        cols = slice(l * 128, l * 128 + 128)
        logits.append(SCALE * (e_out[3, :, cols] + e_in[0, :, cols] + e_in[1, :, cols] + e_in[2, :, cols]))
    top = fold([jnp.max(v, axis=0, keepdims=True) for v in logits], jnp.maximum, low)
    expo = [jnp.exp(v - t) for v, t in zip(logits, top)]
    total = fold([jnp.sum(v, axis=0, keepdims=True) for v in expo], jnp.add, 0.0)
    for l in range(7):
        rows = [jnp.sum(expo[l][s * 8:s * 8 + 8, :], axis=0, keepdims=True) for s in range(4)]
        weight = jnp.concatenate(rows + rows, axis=0) / total[l]
        if l == 6:
            weight = jnp.where(lane1 < PART, weight, 0.0)
        wb[3, :, l * 128:l * 128 + 128] = weight

    def weight_copy(dz):
        p = pos_of(-dz)
        return remote(wb.at[3], wb.at[p], ww_send.at[p], ww_recv.at[p], zdev(dz))

    for dz in (2, 1, 3):
        weight_copy(dz).start()
    def spread(p, first):
        for l in range(7):
            cols = slice(l * 128, l * 128 + 128)
            cls = [jnp.broadcast_to(cb[p, s:s + 1, cols], (8, 128)).astype(F32) for s in range(4)]
            val = [jnp.broadcast_to(wb[p, s:s + 1, cols], (8, 128)) for s in range(4)]
            for r in range(0, 256, 16):
                both = []
                for half in (r, r + 8):
                    rows = order[half:half + 8, :]
                    acc = jnp.zeros((8, 128), F32)
                    for s in range(4):
                        acc = jnp.where(cls[s] == rows, val[s], acc)
                    if first and l == 0:
                        totals[half:half + 8, :] = acc
                    else:
                        totals[half:half + 8, :] += acc
                    both.append(acc)
                wt[r:r + 16, p * ROWS + l * 128:p * ROWS + l * 128 + 128] = jnp.concatenate(both, axis=0).astype(BF16)

    spread(3, True)
    for dz in (1, 3, 2):
        weight_copy(dz).wait_recv()
        spread(pos_of(-dz), False)

    extra = []
    for i in range(16):
        column = jnp.broadcast_to(jnp.sum(totals[i * 16:i * 16 + 16, :], axis=1, keepdims=True), (16, 128))
        line = jnp.sum(jnp.where(row_id == lane_id, column, 0.0), axis=0, keepdims=True)
        high = line.astype(BF16).astype(F32)
        low = line - high
        extra.append(jnp.where(row_id == 12, high, jnp.where(row_id == 13, low, 0.0)))
    extra = jnp.concatenate(extra, axis=0)

    wide_row = lax.broadcasted_iota(jnp.int32, (256, 128), 0) % 16
    mine = pl.ds(pl.multiple_of(c * 128, 128), 128)
    theirs = pl.ds(pl.multiple_of((1 - c) * 128, 128), 128)

    def pair_copy(h):
        return remote(pair_out.at[h], pair_in.at[h], pr_send.at[h], pr_recv.at[h], dev(x, y, 1 - c, z))

    for h in (0, 1):
        for j in range(2):
            col = h * HALF + j * 256
            part_sum = jnp.dot(wt[...], sh[:, col:col + 256], preferred_element_type=F32)
            if j == 0:
                sums[h, :, 0:128] = jnp.where(wide_row < 12, part_sum[:, 0:128], extra)
                sums[h, :, 128:256] = part_sum[:, 128:256]
            else:
                sums[h, :, 256:512] = part_sum
        pair_out[h] = sums[h, theirs, :].astype(BF16)
        pair_copy(h).start()

    me16 = x * 4 + y

    def final_copy(i):
        x_, y_ = i // 4, i % 4
        rows = pl.ds(pl.multiple_of(((y_ // 2) * 4 + x_) * 16, 16), 16)
        return remote(msg.at[y_ % 2, rows, :], fin.at[me16], fn_send.at[i], fn_recv.at[me16], dev(x_, y_, c, z))

    def send_final(h, j):
        i = ((x + 2 + j // 2) % 4) * 4 + ((y // 2 + 1 + j) % 2) * 2 + h

        @pl.when(i != me16)
        def _():
            final_copy(i).start()

        return 0

    for h in (0, 1):
        pair_copy(h).wait_recv()
        both = sums[h, mine, :] + pair_in[h].astype(F32)
        msg[h, :, 128:HALF] = both[:, 128:HALF].astype(BF16)
        first = both[:, 0:128]
        whole = first + pltpu.roll(first, 127, 0)
        high = whole.astype(BF16).astype(F32)
        low = pltpu.roll(whole - high, 1, 0)
        first = jnp.where(wide_row[0:128] == 12, high, jnp.where(wide_row[0:128] == 13, low, first))
        msg[h, :, 0:128] = first.astype(BF16)
        lax.fori_loop(0, 8, lambda j, _: send_final(h, j), 0)

    own_row = pl.ds(pl.multiple_of(((y // 2) * 4 + x) * 16, 16), 16)
    fin[me16] = msg[y % 2, own_row, :]

    def wait_final(i, _):
        @pl.when(i != me16)
        def _():
            remote(fin.at[i], fin.at[i], fn_send.at[i], fn_recv.at[i], dev(x, y, 1 - c, z)).wait_recv()

        return 0

    lax.fori_loop(0, 16, wait_final, 0)

    acc = fin[0].astype(F32)
    for i in range(1, 16):
        acc = acc + fin[i].astype(F32)
    line = acc[12:13, 0:128] + acc[13:14, 0:128]
    den = jnp.sum(jnp.where(row_id == lane_id, jnp.broadcast_to(line, (16, 128)), 0.0), axis=1, keepdims=True) + 1.0
    out[...] = (acc / den)[0:12, :]

    for dc, dz in stage_offsets:
        stage_copy(dc, dz).wait_send()
    for dz in (1, 2, 3):
        for h in (0, 1):
            part_copy(dz, h).wait_send()
        cand_copy(dz).wait_send()
        weight_copy(dz).wait_send()
    for k in (1, 2, 3):
        for a in range(4):
            second_send(a, k).wait_send()
    for a in range(4):
        for b_ in range(4):
            sib_copy(a, b_).wait_send()
    for p in range(3):
        rs_copy(p).wait_send()

    def left_final(i, _):
        @pl.when(i != me16)
        def _():
            final_copy(i).wait_send()

        return 0

    lax.fori_loop(0, 16, left_final, 0)
    for h in (0, 1):
        pair_copy(h).wait_send()


def on_device(particles, references, candidates, shifts, class_order):
    dma = pltpu.SemaphoreType.DMA
    return pl.pallas_call(
        kernel,
        out_shape=jax.ShapeDtypeStruct((12, HALF), F32),
        in_specs=[
            pl.BlockSpec(memory_space=pl.ANY),
            pl.BlockSpec(memory_space=pl.ANY),
            pl.BlockSpec(memory_space=pl.ANY),
            pl.BlockSpec(memory_space=pltpu.SMEM),
            pl.BlockSpec(memory_space=pl.ANY),
        ],
        out_specs=pl.BlockSpec(memory_space=pltpu.VMEM),
        scratch_shapes=[
            pltpu.VMEM((12, 4096), BF16),
            pltpu.VMEM((PART, 4096), BF16),
            pltpu.VMEM((8, 12, HALF), BF16),
            pltpu.VMEM((96, HALF), F32),
            pltpu.VMEM((2, REFS, HALF), BF16),
            pltpu.VMEM((2, CLS, ROT, HALF), F32),
            pltpu.VMEM((2, CLS, ROT, 128), F32),
            pltpu.VMEM((CLS, ROT, 128), F32),
            pltpu.VMEM((3, 2, PART, HALF), BF16),
            pltpu.VMEM((2, 16, HALF), F32),
            pltpu.VMEM((4 * ROWS, 2 * HALF), BF16),
            pltpu.VMEM((4, PART), jnp.int32),
            pltpu.VMEM((4, 8, ROWS), jnp.int32),
            pltpu.SMEM((4, 8, 128), jnp.int32),
            pltpu.VMEM((1, CLS), jnp.int32),
            pltpu.VMEM((256, 128), F32),
            pltpu.VMEM((512, 2 * HALF), BF16),
            pltpu.VMEM((512, 2 * HALF), BF16),
            pltpu.VMEM((4, 32, ROWS), F32),
            pltpu.VMEM((3, 32, ROWS), F32),
            pltpu.VMEM((4, 8, ROWS), F32),
            pltpu.VMEM((256, 4 * ROWS), BF16),
            pltpu.VMEM((256, 128), F32),
            pltpu.VMEM((2, 256, HALF), F32),
            pltpu.VMEM((2, 128, HALF), BF16),
            pltpu.VMEM((2, 128, HALF), BF16),
            pltpu.VMEM((2, 128, HALF), BF16),
            pltpu.VMEM((16, 16, HALF), BF16),
            dma((8,)),
            dma((8,)), dma((8,)), dma((8,)), dma((8,)), dma((4,)), dma((4,)),
            dma((16,)), dma((16,)), dma((16,)), dma((16,)), dma((3,)), dma((3,)),
            dma((3,)), dma((3,)), dma((2,)), dma((2,)), dma((16,)), dma((16,)),
        ],
        compiler_params=pltpu.CompilerParams(
            collective_id=0, has_side_effects=True, vmem_limit_bytes=int(53.8 * 2**20)),
        name="estep",
    )(particles, references, candidates.T, shifts.T, class_order.reshape(1, CLS))


def solution(mesh):
    return jax.shard_map(
        on_device,
        mesh=mesh,
        in_specs=(
            P(("blk", "grp"), None),
            P(("blk", "grp"), None),
            P(("blk", "grp"), None),
            P(),
            P(),
        ),
        out_specs=P("blk", "grp"),
        check_vma=False,
    )
```

```python
import math

import jax
import jax.numpy as jnp
from jax import lax
from jax.experimental import pallas as pl
from jax.experimental.pallas import tpu as pltpu
from jax.sharding import PartitionSpec as P

BOX = 128
ROT = 8
SCALE = 0.05
HALF = 512
PART = 96
TRANS = 9
ROWS = 896
CLS = 192
REFS = 1536
ORDER = (2, 1, 3, 0)
NT = (((1,), (1,)), ((), ()))
F32 = jnp.float32
BF16 = jnp.bfloat16


def pos_of(offset):
    return ORDER.index(offset % 4)


def kernel(
    parts, refs_in, cand_in, shifts, order_in, out,
    refs_own, parts_own, stage, stage32, refs, refs32, squares, hn, pb, table, sh, cand, cb, cs, order_row, order,
    gather_a, gather_b, e_out, e_in, wb, wt, totals, sums, pair_out, pair_in, msg, fin,
    in_sem, st_send, st_recv, pt_send, pt_recv, cd_send, cd_recv,
    ag_send, ag_recv, sb_send, sb_recv, rs_send, rs_recv, ww_send, ww_recv, pr_send, pr_recv, fn_send, fn_recv,
):
    b = lax.axis_index("blk")
    g = lax.axis_index("grp")
    c = b % 2
    x = (b // 2) % 4
    y = (b // 8) * 2 + g // 4
    z = g % 4

    def dev(x_, y_, c_, z_):
        return (((y_ // 2) * 4 + x_) * 2 + c_, (y_ % 2) * 4 + z_)

    def remote(src, dst, ssem, rsem, device):
        return pltpu.make_async_remote_copy(
            src_ref=src, dst_ref=dst, send_sem=ssem, recv_sem=rsem,
            device_id=device, device_id_type=pl.DeviceIdType.MESH)

    def zdev(delta):
        return dev(x, y, c, (z + delta) % 4)

    def shift_tables():
        index = lax.broadcasted_iota(jnp.int32, (16, HALF), 1) + z * HALF
        row = lax.broadcasted_iota(jnp.int32, (16, HALF), 0)
        turns = jnp.zeros((16, HALF), jnp.int32)
        for t in range(TRANS):
            line = shifts[0, t] * (index % (BOX // 2)) + shifts[1, t] * (index // (BOX // 2))
            turns = jnp.where(row == t, line, turns)
        angle = (turns & (BOX - 1)).astype(F32) * (2.0 * math.pi / BOX)
        table[0] = jnp.cos(angle)
        table[1] = jnp.sin(angle)

    def shift_block(p):
        base = p * ROWS
        sh[base + TRANS * PART:base + ROWS, :] = jnp.zeros((ROWS - TRANS * PART, 2 * HALF), BF16)

        def group(q, _):
            rows = pl.ds(pl.multiple_of(q * 16, 16), 16)
            if p == 3:
                re = parts_own[rows, pl.ds(pl.multiple_of(z * HALF, HALF), HALF)].astype(F32)
                im = parts_own[rows, pl.ds(pl.multiple_of(2048 + z * HALF, HALF), HALF)].astype(F32)
            else:
                re = pb[p, 0, rows, :].astype(F32)
                im = pb[p, 1, rows, :].astype(F32)
            for t in range(TRANS):
                co = table[0, t:t + 1, :]
                si = table[1, t:t + 1, :]
                row = base + q * 128 + t * 16 if t < 8 else base + 768 + q * 16
                dst = pl.ds(pl.multiple_of(row, 16), 16)
                sh[dst, 0:HALF] = (re * co - im * si).astype(BF16)
                sh[dst, HALF:2 * HALF] = (re * si + im * co).astype(BF16)
            return 0

        lax.fori_loop(0, 6, group, 0)

    barrier = pltpu.get_barrier_semaphore()

    def greet(device):
        pl.semaphore_signal(barrier, inc=1, device_id=device, device_id_type=pl.DeviceIdType.MESH)

    for k in (1, 2, 3):
        greet(dev((x + k) % 4, y, c, z))
        greet(dev(x, (y + k) % 4, c, z))
    for dz in (1, 2, 3):
        for dc in (0, 1):
            greet(dev(x, y, (c + dc) % 2, (z + dz) % 4))
    greet(dev(x, y, 1 - c, z))
    load_cand = pltpu.make_async_copy(cand_in, cand, in_sem.at[0])
    load_cand.start()
    load_order = pltpu.make_async_copy(order_in, order_row, in_sem.at[1])
    load_order.start()

    load_refs = pltpu.make_async_copy(refs_in, refs_own, in_sem.at[6])
    load_refs.start()
    load_parts = pltpu.make_async_copy(parts, parts_own, in_sem.at[7])
    load_parts.start()

    load_refs.wait()
    pl.semaphore_wait(barrier, 13)

    def stage_copy(dc, dz):
        k = dc * 4 + dz
        c_ = (c + dc) % 2
        z_ = (z + dz) % 4
        cols = pl.ds(pl.multiple_of(c_ * 2048 + z_ * 512, 512), 512)
        return remote(refs_own.at[:, cols], stage.at[c * 4 + z], st_send.at[k], st_recv.at[k],
                      dev(x, y, c_, z_))

    stage_offsets = [(dc, dz) for dz in (2, 1, 3, 0) for dc in (0, 1) if dc or dz]
    for dc, dz in stage_offsets:
        stage_copy(dc, dz).start()
    own_cols = pl.ds(pl.multiple_of(c * 2048 + z * 512, 512), 512)
    stage[c * 4 + z] = refs_own[:, own_cols]

    def part_copy(dz, h):
        z_ = (z + dz) % 4
        cols = pl.ds(pl.multiple_of(h * 2048 + z_ * 512, 512), 512)
        p = pos_of(-dz)
        return remote(parts_own.at[:, cols], pb.at[p, h], pt_send.at[p * 2 + h], pt_recv.at[p * 2 + h], zdev(dz))

    def cand_copy(dz):
        p = pos_of(-dz)
        return remote(cb.at[3], cb.at[p], cd_send.at[p], cd_recv.at[p], zdev(dz))

    for dc, dz in stage_offsets:
        stage_copy(dc, dz).wait_recv()
    for i in range(8):
        stage32[i * 12:(i + 1) * 12, :] = stage[i].astype(F32)

    def block_rows(x_, y_):
        return pl.ds(pl.multiple_of((x_ * 4 + y_) * 96, 96), 96)

    refs[c, block_rows(x, y), :] = stage32[...].astype(BF16)

    def at(a, b_, core=None):
        core = c if core is None else core
        dx = a * (1 - core) + b_ * core
        dy = b_ * (1 - core) + a * core
        return (x + dx) % 4, (y + dy) % 4

    def ref_block(a, b_):
        x_, y_ = at(a, b_)
        return refs.at[c, block_rows(x_, y_), :]

    def first_send(k):
        x_, y_ = at(k, 0)
        block = ref_block(0, 0)
        return remote(block, block, ag_send.at[k], ag_recv.at[((-k) % 4) * 4], dev(x_, y_, c, z))

    def second_send(a, k):
        x_, y_ = at(0, k)
        block = ref_block(a, 0)
        return remote(block, block, ag_send.at[3 + a * 3 + k], ag_recv.at[a * 4 + (-k) % 4], dev(x_, y_, c, z))

    def recv_block(a, b_):
        block = ref_block(a, b_)
        remote(block, block, ag_send.at[0], ag_recv.at[a * 4 + b_], dev(x, y, 1 - c, z)).wait_recv()

    def sib_copy(a, b_):
        block = ref_block(a, b_)
        return remote(block, block, sb_send.at[a * 4 + b_], sb_recv.at[a * 4 + b_], dev(x, y, 1 - c, z))

    for k in (2, 1, 3):
        first_send(k).start()
    sib_copy(0, 0).start()
    load_parts.wait()
    for dz in (1, 3, 2):
        for h in (0, 1):
            part_copy(dz, h).start()
    load_cand.wait()
    own = cand[...]
    lanes = [jnp.concatenate([own[:, q * 16:q * 16 + 16]] * 8, axis=1) for q in range(6)]
    lanes.append(jnp.concatenate([own, jnp.full((4, 32), -1, jnp.int32)], axis=1))
    cb[3, 0:4, :] = jnp.concatenate(lanes, axis=1)
    for dz in (1, 3, 2):
        cand_copy(dz).start()

    shift_tables()
    shift_block(3)
    for k in (2, 1, 3):
        first_send(k).wait_send()
    for k in (2, 1, 3):
        second_send(0, k).start()

    def widen(h, x_, y_, finish=False):
        for core in (0, 1):
            src = pl.ds(pl.multiple_of((x_ * 4 + y_) * 96 + core * 48, 48), 48)
            dst = pl.ds(((((y_ // 2) * 4 + x_) * 2 + core) * 2 + y_ % 2) * 6, 6)
            acc = jnp.zeros((48, 128), F32)
            for j in range(HALF // 128):
                v = refs[h, src, j * 128:(j + 1) * 128].astype(F32)
                refs32[h, dst, :, j * 128:(j + 1) * 128] = v.reshape(6, ROT, 128)
                acc = acc + v * v
            acc = acc.reshape(6, ROT, 128)
            if finish:
                total = 0.5 * jnp.sum(squares[dst] + acc, axis=2, keepdims=True)
                hn[dst] = jnp.broadcast_to(total, (6, ROT, 128))
            else:
                squares[dst] = acc

    for a in (1, 3, 2):
        recv_block(a, 0)
        for k in (2, 1, 3):
            second_send(a, k).start()
        sib_copy(a, 0).start()
    for a in range(4):
        widen(c, *at(a, 0))
    for b_ in (1, 3, 2):
        recv_block(0, b_)
        sib_copy(0, b_).start()
        widen(c, *at(0, b_))

    load_order.wait()
    row_id = lax.broadcasted_iota(jnp.int32, (16, 128), 0)
    lane_id = lax.broadcasted_iota(jnp.int32, (16, 128), 1)
    first = jnp.broadcast_to(order_row[:, 0:128], (16, 128)).astype(F32)
    rest_order = jnp.concatenate([order_row[:, 128:CLS], jnp.full((1, 256 - CLS), -1, jnp.int32)], axis=1)
    second = jnp.broadcast_to(rest_order, (16, 128)).astype(F32)
    for i in range(16):
        start = ((i % 8) * 2 + i // 8) * 12
        here = jnp.where(lane_id == start + row_id, first, 0.0)
        here = here + jnp.where(lane_id + 128 == start + row_id, second, 0.0)
        column = jnp.broadcast_to(jnp.sum(here, axis=1, keepdims=True), (16, 128))
        order[i * 16:i * 16 + 16, :] = jnp.where(row_id < 12, column, -2.0)

    for dz in (1, 3, 2):
        for h in (0, 1):
            part_copy(dz, h).wait_recv()
        cand_copy(dz).wait_recv()
        shift_block(pos_of(-dz))
        for b_ in (1, 3, 2):
            recv_block(dz, b_)
            sib_copy(dz, b_).start()
            widen(c, *at(dz, b_))
    for p in range(4):
        pltpu.make_async_copy(cb.at[p, :, pl.ds(768, 128)], cs.at[p], in_sem.at[2 + p]).start()
    arrivals = [(a, 0) for a in (0, 1, 3, 2)] + [(0, b_) for b_ in (1, 3, 2)]
    arrivals += [(a, b_) for a in (1, 3, 2) for b_ in (1, 3, 2)]
    for a, b_ in arrivals:
        sib_copy(a, b_).wait_recv()
        widen(1 - c, *at(a, b_, 1 - c), True)
    for p in range(4):
        pltpu.make_async_copy(cb.at[p, :, pl.ds(768, 128)], cs.at[p], in_sem.at[2 + p]).wait()

    def rs_copy(p):
        return remote(e_out.at[p], e_in.at[p], rs_send.at[p], rs_recv.at[p], zdev(ORDER[p]))

    def gather(dst, p, q):
        for i in range(16):
            for s in (0, 2):
                first = cs[p, s, q * 16 + i]
                second = cs[p, s + 1, q * 16 + i]
                row = i * 32 + s * 8
                for h in (0, 1):
                    both = jnp.concatenate([refs32[h, first], refs32[h, second]], axis=0)
                    dst[row:row + 16, h * HALF:(h + 1) * HALF] = both.astype(BF16)

    tile_lane = lax.broadcasted_iota(jnp.int32, (8, 128), 1)

    def score(src, p, q, last):
        base = p * ROWS
        moved = jnp.concatenate(
            [sh[pl.ds(pl.multiple_of(base + q * 128, 128), 128), :],
             sh[pl.ds(pl.multiple_of(base + 768, 128), 128), :]], axis=0)
        raw = lax.dot_general(src[...], moved, NT, preferred_element_type=F32)
        main = [jnp.zeros((8, 128), F32) for _ in range(4)]
        for i in range(16):
            in_main = (tile_lane & 15) == i
            in_last = tile_lane == q * 16 + i
            for s in range(4):
                row = i * 32 + s * 8
                norm = hn[cs[p, s, q * 16 + i]]
                main[s] = jnp.where(in_main, raw[row:row + 8, 0:128] - norm, main[s])
                last[s] = jnp.where(in_last, raw[row:row + 8, 128:256] - norm, last[s])
        for s in range(4):
            e_out[p, s * 8:s * 8 + 8, q * 128:q * 128 + 128] = main[s]
        return last

    gather(gather_a, 0, 0)

    def scores(p, _):
        last = [jnp.zeros((8, 128), F32) for _ in range(4)]
        for q in range(6):
            here, ahead = (gather_a, gather_b) if q % 2 == 0 else (gather_b, gather_a)
            if q < 5:
                gather(ahead, p, q + 1)
            else:
                gather(ahead, jnp.minimum(p + 1, 3), 0)
            last = score(here, p, q, last)
        for s in range(4):
            e_out[p, s * 8:s * 8 + 8, 768:896] = last[s]
        for k in range(3):
            @pl.when(p == k)
            def _():
                rs_copy(k).start()
        return 0

    lax.fori_loop(0, 4, scores, 0)

    for p in range(3):
        rs_copy(p).wait_recv()
    low = -1e30
    lane1 = lax.broadcasted_iota(jnp.int32, (8, 128), 1)
    row1 = lax.broadcasted_iota(jnp.int32, (8, 128), 0)

    def fold(rows, op, fill):
        wide = jnp.concatenate(rows[0:6] + [rows[5], rows[5]], axis=0)
        for step in (64, 32, 16):
            wide = op(wide, pltpu.roll(wide, step, 1))
        shifted = [rows[6]] + [pltpu.roll(rows[6], 128 - 16 * q, 1) for q in range(1, 6)]
        rest = jnp.concatenate(shifted + [shifted[5], shifted[5]], axis=0)
        rest = jnp.where(lane1 < 16, rest, fill)
        for step in (16, 32, 64):
            rest = op(rest, pltpu.roll(rest, step, 1))
        wide = op(wide, rest)
        final = jnp.sum(jnp.where((lane1 >> 4) == row1, wide, 0.0), axis=0, keepdims=True)
        return [wide[q:q + 1, :] for q in range(6)] + [final]

    logits = []
    for l in range(7):
        cols = slice(l * 128, l * 128 + 128)
        logits.append(SCALE * (e_out[3, :, cols] + e_in[0, :, cols] + e_in[1, :, cols] + e_in[2, :, cols]))
    top = fold([jnp.max(v, axis=0, keepdims=True) for v in logits], jnp.maximum, low)
    expo = [jnp.exp(v - t) for v, t in zip(logits, top)]
    total = fold([jnp.sum(v, axis=0, keepdims=True) for v in expo], jnp.add, 0.0)
    for l in range(7):
        rows = [jnp.sum(expo[l][s * 8:s * 8 + 8, :], axis=0, keepdims=True) for s in range(4)]
        weight = jnp.concatenate(rows + rows, axis=0) / total[l]
        if l == 6:
            weight = jnp.where(lane1 < PART, weight, 0.0)
        wb[3, :, l * 128:l * 128 + 128] = weight

    def weight_copy(dz):
        p = pos_of(-dz)
        return remote(wb.at[3], wb.at[p], ww_send.at[p], ww_recv.at[p], zdev(dz))

    for dz in (2, 1, 3):
        weight_copy(dz).start()
    def spread(p, first):
        for l in range(7):
            cols = slice(l * 128, l * 128 + 128)
            cls = [jnp.broadcast_to(cb[p, s:s + 1, cols], (8, 128)).astype(F32) for s in range(4)]
            val = [jnp.broadcast_to(wb[p, s:s + 1, cols], (8, 128)) for s in range(4)]
            for r in range(0, 256, 16):
                both = []
                for half in (r, r + 8):
                    rows = order[half:half + 8, :]
                    acc = jnp.zeros((8, 128), F32)
                    for s in range(4):
                        acc = jnp.where(cls[s] == rows, val[s], acc)
                    if first and l == 0:
                        totals[half:half + 8, :] = acc
                    else:
                        totals[half:half + 8, :] += acc
                    both.append(acc)
                wt[r:r + 16, p * ROWS + l * 128:p * ROWS + l * 128 + 128] = jnp.concatenate(both, axis=0).astype(BF16)

    spread(3, True)
    for dz in (1, 3, 2):
        weight_copy(dz).wait_recv()
        spread(pos_of(-dz), False)

    extra = []
    for i in range(16):
        column = jnp.broadcast_to(jnp.sum(totals[i * 16:i * 16 + 16, :], axis=1, keepdims=True), (16, 128))
        line = jnp.sum(jnp.where(row_id == lane_id, column, 0.0), axis=0, keepdims=True)
        high = line.astype(BF16).astype(F32)
        low = line - high
        extra.append(jnp.where(row_id == 12, high, jnp.where(row_id == 13, low, 0.0)))
    extra = jnp.concatenate(extra, axis=0)

    wide_row = lax.broadcasted_iota(jnp.int32, (256, 128), 0) % 16
    mine = pl.ds(pl.multiple_of(c * 128, 128), 128)
    theirs = pl.ds(pl.multiple_of((1 - c) * 128, 128), 128)

    def pair_copy(h):
        return remote(pair_out.at[h], pair_in.at[h], pr_send.at[h], pr_recv.at[h], dev(x, y, 1 - c, z))

    for h in (0, 1):
        for j in range(2):
            col = h * HALF + j * 256
            part_sum = jnp.dot(wt[...], sh[:, col:col + 256], preferred_element_type=F32)
            if j == 0:
                sums[h, :, 0:128] = jnp.where(wide_row < 12, part_sum[:, 0:128], extra)
                sums[h, :, 128:256] = part_sum[:, 128:256]
            else:
                sums[h, :, 256:512] = part_sum
        pair_out[h] = sums[h, theirs, :].astype(BF16)
        pair_copy(h).start()

    me16 = x * 4 + y

    def final_copy(i):
        x_, y_ = i // 4, i % 4
        rows = pl.ds(pl.multiple_of(((y_ // 2) * 4 + x_) * 16, 16), 16)
        return remote(msg.at[y_ % 2, rows, :], fin.at[me16], fn_send.at[i], fn_recv.at[me16], dev(x_, y_, c, z))

    def send_final(h, j):
        i = ((x + 2 + j // 2) % 4) * 4 + ((y // 2 + 1 + j) % 2) * 2 + h

        @pl.when(i != me16)
        def _():
            final_copy(i).start()

        return 0

    for h in (0, 1):
        pair_copy(h).wait_recv()
        both = sums[h, mine, :] + pair_in[h].astype(F32)
        msg[h, :, 128:HALF] = both[:, 128:HALF].astype(BF16)
        first = both[:, 0:128]
        whole = first + pltpu.roll(first, 127, 0)
        high = whole.astype(BF16).astype(F32)
        low = pltpu.roll(whole - high, 1, 0)
        first = jnp.where(wide_row[0:128] == 12, high, jnp.where(wide_row[0:128] == 13, low, first))
        msg[h, :, 0:128] = first.astype(BF16)
        lax.fori_loop(0, 8, lambda j, _: send_final(h, j), 0)

    own_row = pl.ds(pl.multiple_of(((y // 2) * 4 + x) * 16, 16), 16)
    fin[me16] = msg[y % 2, own_row, :]

    def wait_final(i, _):
        @pl.when(i != me16)
        def _():
            remote(fin.at[i], fin.at[i], fn_send.at[i], fn_recv.at[i], dev(x, y, 1 - c, z)).wait_recv()

        return 0

    lax.fori_loop(0, 16, wait_final, 0)

    acc = fin[0].astype(F32)
    for i in range(1, 16):
        acc = acc + fin[i].astype(F32)
    line = acc[12:13, 0:128] + acc[13:14, 0:128]
    den = jnp.sum(jnp.where(row_id == lane_id, jnp.broadcast_to(line, (16, 128)), 0.0), axis=1, keepdims=True) + 1.0
    out[...] = (acc / den)[0:12, :]

    for dc, dz in stage_offsets:
        stage_copy(dc, dz).wait_send()
    for dz in (1, 2, 3):
        for h in (0, 1):
            part_copy(dz, h).wait_send()
        cand_copy(dz).wait_send()
        weight_copy(dz).wait_send()
    for k in (1, 2, 3):
        for a in range(4):
            second_send(a, k).wait_send()
    for a in range(4):
        for b_ in range(4):
            sib_copy(a, b_).wait_send()
    for p in range(3):
        rs_copy(p).wait_send()

    def left_final(i, _):
        @pl.when(i != me16)
        def _():
            final_copy(i).wait_send()

        return 0

    lax.fori_loop(0, 16, left_final, 0)
    for h in (0, 1):
        pair_copy(h).wait_send()


def on_device(particles, references, candidates, shifts, class_order):
    dma = pltpu.SemaphoreType.DMA
    return pl.pallas_call(
        kernel,
        out_shape=jax.ShapeDtypeStruct((12, HALF), F32),
        in_specs=[
            pl.BlockSpec(memory_space=pl.ANY),
            pl.BlockSpec(memory_space=pl.ANY),
            pl.BlockSpec(memory_space=pl.ANY),
            pl.BlockSpec(memory_space=pltpu.SMEM),
            pl.BlockSpec(memory_space=pl.ANY),
        ],
        out_specs=pl.BlockSpec(memory_space=pltpu.VMEM),
        scratch_shapes=[
            pltpu.VMEM((12, 4096), BF16),
            pltpu.VMEM((PART, 4096), BF16),
            pltpu.VMEM((8, 12, HALF), BF16),
            pltpu.VMEM((96, HALF), F32),
            pltpu.VMEM((2, REFS, HALF), BF16),
            pltpu.VMEM((2, CLS, ROT, HALF), F32),
            pltpu.VMEM((CLS, ROT, 128), F32),
            pltpu.VMEM((CLS, ROT, 128), F32),
            pltpu.VMEM((3, 2, PART, HALF), BF16),
            pltpu.VMEM((2, 16, HALF), F32),
            pltpu.VMEM((4 * ROWS, 2 * HALF), BF16),
            pltpu.VMEM((4, PART), jnp.int32),
            pltpu.VMEM((4, 8, ROWS), jnp.int32),
            pltpu.SMEM((4, 8, 128), jnp.int32),
            pltpu.VMEM((1, CLS), jnp.int32),
            pltpu.VMEM((256, 128), F32),
            pltpu.VMEM((512, 2 * HALF), BF16),
            pltpu.VMEM((512, 2 * HALF), BF16),
            pltpu.VMEM((4, 32, ROWS), F32),
            pltpu.VMEM((3, 32, ROWS), F32),
            pltpu.VMEM((4, 8, ROWS), F32),
            pltpu.VMEM((256, 4 * ROWS), BF16),
            pltpu.VMEM((256, 128), F32),
            pltpu.VMEM((2, 256, HALF), F32),
            pltpu.VMEM((2, 128, HALF), BF16),
            pltpu.VMEM((2, 128, HALF), BF16),
            pltpu.VMEM((2, 128, HALF), BF16),
            pltpu.VMEM((16, 16, HALF), BF16),
            dma((8,)),
            dma((8,)), dma((8,)), dma((8,)), dma((8,)), dma((4,)), dma((4,)),
            dma((16,)), dma((16,)), dma((16,)), dma((16,)), dma((3,)), dma((3,)),
            dma((3,)), dma((3,)), dma((2,)), dma((2,)), dma((16,)), dma((16,)),
        ],
        compiler_params=pltpu.CompilerParams(
            collective_id=0, has_side_effects=True, vmem_limit_bytes=int(53.8 * 2**20)),
        name="estep",
    )(particles, references, candidates.T, shifts.T, class_order.reshape(1, CLS))


def solution(mesh):
    return jax.shard_map(
        on_device,
        mesh=mesh,
        in_specs=(
            P(("blk", "grp"), None),
            P(("blk", "grp"), None),
            P(("blk", "grp"), None),
            P(),
            P(),
        ),
        out_specs=P("blk", "grp"),
        check_vma=False,
    )
```

```python
import math

import jax
import jax.numpy as jnp
from jax import lax
from jax.experimental import pallas as pl
from jax.experimental.pallas import tpu as pltpu
from jax.sharding import PartitionSpec as P

BOX = 128
ROT = 8
SCALE = 0.05
HALF = 512
PART = 96
TRANS = 9
ROWS = 896
CLS = 192
REFS = 1536
ORDER = (2, 1, 3, 0)
NT = (((1,), (1,)), ((), ()))
F32 = jnp.float32
BF16 = jnp.bfloat16


def pos_of(offset):
    return ORDER.index(offset % 4)


def kernel(
    parts, refs_in, cand_in, shifts, order_in, out,
    refs_own, parts_own, stage, stage32, refs, refs32, squares, hn, pb, table, sh, cand, cb, cs, order_row, order,
    gather_a, gather_b, e_out, e_in, wb, wt, totals, sums, pair_out, pair_in, msg, fin,
    in_sem, st_send, st_recv, pt_send, pt_recv, cd_send, cd_recv,
    ag_send, ag_recv, sb_send, sb_recv, rs_send, rs_recv, ww_send, ww_recv, pr_send, pr_recv, fn_send, fn_recv,
):
    b = lax.axis_index("blk")
    g = lax.axis_index("grp")
    c = b % 2
    x = (b // 2) % 4
    y = (b // 8) * 2 + g // 4
    z = g % 4

    def dev(x_, y_, c_, z_):
        return (((y_ // 2) * 4 + x_) * 2 + c_, (y_ % 2) * 4 + z_)

    def remote(src, dst, ssem, rsem, device):
        return pltpu.make_async_remote_copy(
            src_ref=src, dst_ref=dst, send_sem=ssem, recv_sem=rsem,
            device_id=device, device_id_type=pl.DeviceIdType.MESH)

    def zdev(delta):
        return dev(x, y, c, (z + delta) % 4)

    def shift_tables():
        index = lax.broadcasted_iota(jnp.int32, (16, HALF), 1) + z * HALF
        row = lax.broadcasted_iota(jnp.int32, (16, HALF), 0)
        turns = jnp.zeros((16, HALF), jnp.int32)
        for t in range(TRANS):
            line = shifts[0, t] * (index % (BOX // 2)) + shifts[1, t] * (index // (BOX // 2))
            turns = jnp.where(row == t, line, turns)
        angle = (turns & (BOX - 1)).astype(F32) * (2.0 * math.pi / BOX)
        table[0] = jnp.cos(angle)
        table[1] = jnp.sin(angle)

    def shift_block(p):
        base = p * ROWS
        sh[base + TRANS * PART:base + ROWS, :] = jnp.zeros((ROWS - TRANS * PART, 2 * HALF), BF16)

        def group(q, _):
            rows = pl.ds(pl.multiple_of(q * 16, 16), 16)
            if p == 3:
                re = parts_own[rows, pl.ds(pl.multiple_of(z * HALF, HALF), HALF)].astype(F32)
                im = parts_own[rows, pl.ds(pl.multiple_of(2048 + z * HALF, HALF), HALF)].astype(F32)
            else:
                re = pb[p, 0, rows, :].astype(F32)
                im = pb[p, 1, rows, :].astype(F32)
            for t in range(TRANS):
                co = table[0, t:t + 1, :]
                si = table[1, t:t + 1, :]
                row = base + q * 128 + t * 16 if t < 8 else base + 768 + q * 16
                dst = pl.ds(pl.multiple_of(row, 16), 16)
                sh[dst, 0:HALF] = (re * co - im * si).astype(BF16)
                sh[dst, HALF:2 * HALF] = (re * si + im * co).astype(BF16)
            return 0

        lax.fori_loop(0, 6, group, 0)

    barrier = pltpu.get_barrier_semaphore()

    def greet(device):
        pl.semaphore_signal(barrier, inc=1, device_id=device, device_id_type=pl.DeviceIdType.MESH)

    for k in (1, 2, 3):
        greet(dev((x + k) % 4, y, c, z))
        greet(dev(x, (y + k) % 4, c, z))
    for dz in (1, 2, 3):
        for dc in (0, 1):
            greet(dev(x, y, (c + dc) % 2, (z + dz) % 4))
    greet(dev(x, y, 1 - c, z))
    load_cand = pltpu.make_async_copy(cand_in, cand, in_sem.at[0])
    load_cand.start()
    load_order = pltpu.make_async_copy(order_in, order_row, in_sem.at[1])
    load_order.start()

    load_refs = pltpu.make_async_copy(refs_in, refs_own, in_sem.at[6])
    load_refs.start()
    load_parts = pltpu.make_async_copy(parts, parts_own, in_sem.at[7])
    load_parts.start()

    load_refs.wait()
    pl.semaphore_wait(barrier, 13)

    def stage_copy(dc, dz):
        k = dc * 4 + dz
        c_ = (c + dc) % 2
        z_ = (z + dz) % 4
        cols = pl.ds(pl.multiple_of(c_ * 2048 + z_ * 512, 512), 512)
        return remote(refs_own.at[:, cols], stage.at[c * 4 + z], st_send.at[k], st_recv.at[k],
                      dev(x, y, c_, z_))

    stage_offsets = [(dc, dz) for dz in (2, 1, 3, 0) for dc in (0, 1) if dc or dz]
    for dc, dz in stage_offsets:
        stage_copy(dc, dz).start()
    own_cols = pl.ds(pl.multiple_of(c * 2048 + z * 512, 512), 512)
    stage[c * 4 + z] = refs_own[:, own_cols]

    def part_copy(dz, h):
        z_ = (z + dz) % 4
        cols = pl.ds(pl.multiple_of(h * 2048 + z_ * 512, 512), 512)
        p = pos_of(-dz)
        return remote(parts_own.at[:, cols], pb.at[p, h], pt_send.at[p * 2 + h], pt_recv.at[p * 2 + h], zdev(dz))

    def cand_copy(dz):
        p = pos_of(-dz)
        return remote(cb.at[3], cb.at[p], cd_send.at[p], cd_recv.at[p], zdev(dz))

    for dc, dz in stage_offsets:
        stage_copy(dc, dz).wait_recv()
    for i in range(8):
        stage32[i * 12:(i + 1) * 12, :] = stage[i].astype(F32)

    def block_rows(x_, y_):
        return pl.ds(pl.multiple_of((x_ * 4 + y_) * 96, 96), 96)

    refs[c, block_rows(x, y), :] = stage32[...].astype(BF16)

    def at(a, b_, core=None):
        core = c if core is None else core
        dx = a * (1 - core) + b_ * core
        dy = b_ * (1 - core) + a * core
        return (x + dx) % 4, (y + dy) % 4

    def ref_block(a, b_):
        x_, y_ = at(a, b_)
        return refs.at[c, block_rows(x_, y_), :]

    def first_send(k):
        x_, y_ = at(k, 0)
        block = ref_block(0, 0)
        return remote(block, block, ag_send.at[k], ag_recv.at[((-k) % 4) * 4], dev(x_, y_, c, z))

    def second_send(a, k):
        x_, y_ = at(0, k)
        block = ref_block(a, 0)
        return remote(block, block, ag_send.at[3 + a * 3 + k], ag_recv.at[a * 4 + (-k) % 4], dev(x_, y_, c, z))

    def recv_block(a, b_):
        block = ref_block(a, b_)
        remote(block, block, ag_send.at[0], ag_recv.at[a * 4 + b_], dev(x, y, 1 - c, z)).wait_recv()

    def sib_copy(a, b_):
        block = ref_block(a, b_)
        return remote(block, block, sb_send.at[a * 4 + b_], sb_recv.at[a * 4 + b_], dev(x, y, 1 - c, z))

    for k in (2, 1, 3):
        first_send(k).start()
    sib_copy(0, 0).start()
    load_parts.wait()
    for dz in (1, 3, 2):
        for h in (0, 1):
            part_copy(dz, h).start()
    load_cand.wait()
    own = cand[...]
    lanes = [jnp.concatenate([own[:, q * 16:q * 16 + 16]] * 8, axis=1) for q in range(6)]
    lanes.append(jnp.concatenate([own, jnp.full((4, 32), -1, jnp.int32)], axis=1))
    cb[3, 0:4, :] = jnp.concatenate(lanes, axis=1)
    for dz in (1, 3, 2):
        cand_copy(dz).start()

    shift_tables()
    shift_block(3)
    for k in (2, 1, 3):
        first_send(k).wait_send()
    for k in (2, 1, 3):
        second_send(0, k).start()

    def widen(h, x_, y_, finish=False):
        for core in (0, 1):
            src = pl.ds(pl.multiple_of((x_ * 4 + y_) * 96 + core * 48, 48), 48)
            dst = pl.ds(((((y_ // 2) * 4 + x_) * 2 + core) * 2 + y_ % 2) * 6, 6)
            acc = jnp.zeros((48, 128), F32)
            for j in range(HALF // 128):
                v = refs[h, src, j * 128:(j + 1) * 128].astype(F32)
                refs32[h, dst, :, j * 128:(j + 1) * 128] = v.reshape(6, ROT, 128)
                acc = acc + v * v
            acc = acc.reshape(6, ROT, 128)
            if finish:
                total = 0.5 * jnp.sum(squares[dst] + acc, axis=2, keepdims=True)
                hn[dst] = jnp.broadcast_to(total, (6, ROT, 128))
            else:
                squares[dst] = acc

    for a in (1, 3, 2):
        recv_block(a, 0)
        for k in (2, 1, 3):
            second_send(a, k).start()
        sib_copy(a, 0).start()
    for a in range(4):
        widen(c, *at(a, 0))
    for b_ in (1, 3, 2):
        recv_block(0, b_)
        sib_copy(0, b_).start()
        widen(c, *at(0, b_))

    load_order.wait()
    row_id = lax.broadcasted_iota(jnp.int32, (16, 128), 0)
    lane_id = lax.broadcasted_iota(jnp.int32, (16, 128), 1)
    first = jnp.broadcast_to(order_row[:, 0:128], (16, 128)).astype(F32)
    rest_order = jnp.concatenate([order_row[:, 128:CLS], jnp.full((1, 256 - CLS), -1, jnp.int32)], axis=1)
    second = jnp.broadcast_to(rest_order, (16, 128)).astype(F32)
    for i in range(16):
        start = ((i % 8) * 2 + i // 8) * 12
        here = jnp.where(lane_id == start + row_id, first, 0.0)
        here = here + jnp.where(lane_id + 128 == start + row_id, second, 0.0)
        column = jnp.broadcast_to(jnp.sum(here, axis=1, keepdims=True), (16, 128))
        order[i * 16:i * 16 + 16, :] = jnp.where(row_id < 12, column, -2.0)

    def take_blocks(a):
        for b_ in (1, 3, 2):
            recv_block(a, b_)
            sib_copy(a, b_).start()
            widen(c, *at(a, b_))

    def take_particles(dz):
        for h in (0, 1):
            part_copy(dz, h).wait_recv()
        cand_copy(dz).wait_recv()
        shift_block(pos_of(-dz))

    take_blocks(1)
    take_particles(1)
    take_blocks(3)
    take_particles(3)
    take_particles(2)
    take_blocks(2)
    for p in range(4):
        pltpu.make_async_copy(cb.at[p, :, pl.ds(768, 128)], cs.at[p], in_sem.at[2 + p]).start()
    arrivals = [(a, 0) for a in (0, 1, 3, 2)] + [(0, b_) for b_ in (1, 3, 2)]
    arrivals += [(a, b_) for a in (1, 3, 2) for b_ in (1, 3, 2)]
    for a, b_ in arrivals:
        sib_copy(a, b_).wait_recv()
        widen(1 - c, *at(a, b_, 1 - c), True)
    for p in range(4):
        pltpu.make_async_copy(cb.at[p, :, pl.ds(768, 128)], cs.at[p], in_sem.at[2 + p]).wait()

    def rs_copy(p):
        return remote(e_out.at[p], e_in.at[p], rs_send.at[p], rs_recv.at[p], zdev(ORDER[p]))

    def gather(dst, p, q):
        for i in range(16):
            for s in (0, 2):
                first = cs[p, s, q * 16 + i]
                second = cs[p, s + 1, q * 16 + i]
                row = i * 32 + s * 8
                for h in (0, 1):
                    both = jnp.concatenate([refs32[h, first], refs32[h, second]], axis=0)
                    dst[row:row + 16, h * HALF:(h + 1) * HALF] = both.astype(BF16)

    tile_lane = lax.broadcasted_iota(jnp.int32, (8, 128), 1)

    def score(src, p, q, last):
        base = p * ROWS
        moved = jnp.concatenate(
            [sh[pl.ds(pl.multiple_of(base + q * 128, 128), 128), :],
             sh[pl.ds(pl.multiple_of(base + 768, 128), 128), :]], axis=0)
        raw = lax.dot_general(src[...], moved, NT, preferred_element_type=F32)
        main = [jnp.zeros((8, 128), F32) for _ in range(4)]
        for i in range(16):
            in_main = (tile_lane & 15) == i
            in_last = tile_lane == q * 16 + i
            for s in range(4):
                row = i * 32 + s * 8
                norm = hn[cs[p, s, q * 16 + i]]
                main[s] = jnp.where(in_main, raw[row:row + 8, 0:128] - norm, main[s])
                last[s] = jnp.where(in_last, raw[row:row + 8, 128:256] - norm, last[s])
        for s in range(4):
            e_out[p, s * 8:s * 8 + 8, q * 128:q * 128 + 128] = main[s]
        return last

    gather(gather_a, 0, 0)

    def scores(p, _):
        last = [jnp.zeros((8, 128), F32) for _ in range(4)]
        for q in range(6):
            here, ahead = (gather_a, gather_b) if q % 2 == 0 else (gather_b, gather_a)
            if q < 5:
                gather(ahead, p, q + 1)
            else:
                gather(ahead, jnp.minimum(p + 1, 3), 0)
            last = score(here, p, q, last)
        for s in range(4):
            e_out[p, s * 8:s * 8 + 8, 768:896] = last[s]
        for k in range(3):
            @pl.when(p == k)
            def _():
                rs_copy(k).start()
        return 0

    lax.fori_loop(0, 4, scores, 0)

    for p in range(3):
        rs_copy(p).wait_recv()
    low = -1e30
    lane1 = lax.broadcasted_iota(jnp.int32, (8, 128), 1)
    row1 = lax.broadcasted_iota(jnp.int32, (8, 128), 0)

    def fold(rows, op, fill):
        wide = jnp.concatenate(rows[0:6] + [rows[5], rows[5]], axis=0)
        for step in (64, 32, 16):
            wide = op(wide, pltpu.roll(wide, step, 1))
        shifted = [rows[6]] + [pltpu.roll(rows[6], 128 - 16 * q, 1) for q in range(1, 6)]
        rest = jnp.concatenate(shifted + [shifted[5], shifted[5]], axis=0)
        rest = jnp.where(lane1 < 16, rest, fill)
        for step in (16, 32, 64):
            rest = op(rest, pltpu.roll(rest, step, 1))
        wide = op(wide, rest)
        final = jnp.sum(jnp.where((lane1 >> 4) == row1, wide, 0.0), axis=0, keepdims=True)
        return [wide[q:q + 1, :] for q in range(6)] + [final]

    logits = []
    for l in range(7):
        cols = slice(l * 128, l * 128 + 128)
        logits.append(SCALE * (e_out[3, :, cols] + e_in[0, :, cols] + e_in[1, :, cols] + e_in[2, :, cols]))
    top = fold([jnp.max(v, axis=0, keepdims=True) for v in logits], jnp.maximum, low)
    expo = [jnp.exp(v - t) for v, t in zip(logits, top)]
    total = fold([jnp.sum(v, axis=0, keepdims=True) for v in expo], jnp.add, 0.0)
    for l in range(7):
        rows = [jnp.sum(expo[l][s * 8:s * 8 + 8, :], axis=0, keepdims=True) for s in range(4)]
        weight = jnp.concatenate(rows + rows, axis=0) / total[l]
        if l == 6:
            weight = jnp.where(lane1 < PART, weight, 0.0)
        wb[3, :, l * 128:l * 128 + 128] = weight

    def weight_copy(dz):
        p = pos_of(-dz)
        return remote(wb.at[3], wb.at[p], ww_send.at[p], ww_recv.at[p], zdev(dz))

    for dz in (2, 1, 3):
        weight_copy(dz).start()
    def spread(p, first):
        for l in range(7):
            cols = slice(l * 128, l * 128 + 128)
            cls = [jnp.broadcast_to(cb[p, s:s + 1, cols], (8, 128)).astype(F32) for s in range(4)]
            val = [jnp.broadcast_to(wb[p, s:s + 1, cols], (8, 128)) for s in range(4)]
            for r in range(0, 256, 16):
                both = []
                for half in (r, r + 8):
                    rows = order[half:half + 8, :]
                    acc = jnp.zeros((8, 128), F32)
                    for s in range(4):
                        acc = jnp.where(cls[s] == rows, val[s], acc)
                    if first and l == 0:
                        totals[half:half + 8, :] = acc
                    else:
                        totals[half:half + 8, :] += acc
                    both.append(acc)
                wt[r:r + 16, p * ROWS + l * 128:p * ROWS + l * 128 + 128] = jnp.concatenate(both, axis=0).astype(BF16)

    spread(3, True)
    for dz in (1, 3, 2):
        weight_copy(dz).wait_recv()
        spread(pos_of(-dz), False)

    extra = []
    for i in range(16):
        column = jnp.broadcast_to(jnp.sum(totals[i * 16:i * 16 + 16, :], axis=1, keepdims=True), (16, 128))
        line = jnp.sum(jnp.where(row_id == lane_id, column, 0.0), axis=0, keepdims=True)
        high = line.astype(BF16).astype(F32)
        low = line - high
        extra.append(jnp.where(row_id == 12, high, jnp.where(row_id == 13, low, 0.0)))
    extra = jnp.concatenate(extra, axis=0)

    wide_row = lax.broadcasted_iota(jnp.int32, (256, 128), 0) % 16
    mine = pl.ds(pl.multiple_of(c * 128, 128), 128)
    theirs = pl.ds(pl.multiple_of((1 - c) * 128, 128), 128)

    def pair_copy(h):
        return remote(pair_out.at[h], pair_in.at[h], pr_send.at[h], pr_recv.at[h], dev(x, y, 1 - c, z))

    for h in (0, 1):
        for j in range(2):
            col = h * HALF + j * 256
            part_sum = jnp.dot(wt[...], sh[:, col:col + 256], preferred_element_type=F32)
            if j == 0:
                sums[h, :, 0:128] = jnp.where(wide_row < 12, part_sum[:, 0:128], extra)
                sums[h, :, 128:256] = part_sum[:, 128:256]
            else:
                sums[h, :, 256:512] = part_sum
        pair_out[h] = sums[h, theirs, :].astype(BF16)
        pair_copy(h).start()

    me16 = x * 4 + y

    def final_copy(i):
        x_, y_ = i // 4, i % 4
        rows = pl.ds(pl.multiple_of(((y_ // 2) * 4 + x_) * 16, 16), 16)
        return remote(msg.at[y_ % 2, rows, :], fin.at[me16], fn_send.at[i], fn_recv.at[me16], dev(x_, y_, c, z))

    def send_final(h, j):
        i = ((x + 2 + j // 2) % 4) * 4 + ((y // 2 + 1 + j) % 2) * 2 + h

        @pl.when(i != me16)
        def _():
            final_copy(i).start()

        return 0

    for h in (0, 1):
        pair_copy(h).wait_recv()
        both = sums[h, mine, :] + pair_in[h].astype(F32)
        msg[h, :, 128:HALF] = both[:, 128:HALF].astype(BF16)
        first = both[:, 0:128]
        whole = first + pltpu.roll(first, 127, 0)
        high = whole.astype(BF16).astype(F32)
        low = pltpu.roll(whole - high, 1, 0)
        first = jnp.where(wide_row[0:128] == 12, high, jnp.where(wide_row[0:128] == 13, low, first))
        msg[h, :, 0:128] = first.astype(BF16)
        lax.fori_loop(0, 8, lambda j, _: send_final(h, j), 0)

    own_row = pl.ds(pl.multiple_of(((y // 2) * 4 + x) * 16, 16), 16)
    fin[me16] = msg[y % 2, own_row, :]

    def wait_final(i, _):
        @pl.when(i != me16)
        def _():
            remote(fin.at[i], fin.at[i], fn_send.at[i], fn_recv.at[i], dev(x, y, 1 - c, z)).wait_recv()

        return 0

    lax.fori_loop(0, 16, wait_final, 0)

    acc = fin[0].astype(F32)
    for i in range(1, 16):
        acc = acc + fin[i].astype(F32)
    line = acc[12:13, 0:128] + acc[13:14, 0:128]
    den = jnp.sum(jnp.where(row_id == lane_id, jnp.broadcast_to(line, (16, 128)), 0.0), axis=1, keepdims=True) + 1.0
    out[...] = (acc / den)[0:12, :]

    for dc, dz in stage_offsets:
        stage_copy(dc, dz).wait_send()
    for dz in (1, 2, 3):
        for h in (0, 1):
            part_copy(dz, h).wait_send()
        cand_copy(dz).wait_send()
        weight_copy(dz).wait_send()
    for k in (1, 2, 3):
        for a in range(4):
            second_send(a, k).wait_send()
    for a in range(4):
        for b_ in range(4):
            sib_copy(a, b_).wait_send()
    for p in range(3):
        rs_copy(p).wait_send()

    def left_final(i, _):
        @pl.when(i != me16)
        def _():
            final_copy(i).wait_send()

        return 0

    lax.fori_loop(0, 16, left_final, 0)
    for h in (0, 1):
        pair_copy(h).wait_send()


def on_device(particles, references, candidates, shifts, class_order):
    dma = pltpu.SemaphoreType.DMA
    return pl.pallas_call(
        kernel,
        out_shape=jax.ShapeDtypeStruct((12, HALF), F32),
        in_specs=[
            pl.BlockSpec(memory_space=pl.ANY),
            pl.BlockSpec(memory_space=pl.ANY),
            pl.BlockSpec(memory_space=pl.ANY),
            pl.BlockSpec(memory_space=pltpu.SMEM),
            pl.BlockSpec(memory_space=pl.ANY),
        ],
        out_specs=pl.BlockSpec(memory_space=pltpu.VMEM),
        scratch_shapes=[
            pltpu.VMEM((12, 4096), BF16),
            pltpu.VMEM((PART, 4096), BF16),
            pltpu.VMEM((8, 12, HALF), BF16),
            pltpu.VMEM((96, HALF), F32),
            pltpu.VMEM((2, REFS, HALF), BF16),
            pltpu.VMEM((2, CLS, ROT, HALF), F32),
            pltpu.VMEM((CLS, ROT, 128), F32),
            pltpu.VMEM((CLS, ROT, 128), F32),
            pltpu.VMEM((3, 2, PART, HALF), BF16),
            pltpu.VMEM((2, 16, HALF), F32),
            pltpu.VMEM((4 * ROWS, 2 * HALF), BF16),
            pltpu.VMEM((4, PART), jnp.int32),
            pltpu.VMEM((4, 8, ROWS), jnp.int32),
            pltpu.SMEM((4, 8, 128), jnp.int32),
            pltpu.VMEM((1, CLS), jnp.int32),
            pltpu.VMEM((256, 128), F32),
            pltpu.VMEM((512, 2 * HALF), BF16),
            pltpu.VMEM((512, 2 * HALF), BF16),
            pltpu.VMEM((4, 32, ROWS), F32),
            pltpu.VMEM((3, 32, ROWS), F32),
            pltpu.VMEM((4, 8, ROWS), F32),
            pltpu.VMEM((256, 4 * ROWS), BF16),
            pltpu.VMEM((256, 128), F32),
            pltpu.VMEM((2, 256, HALF), F32),
            pltpu.VMEM((2, 128, HALF), BF16),
            pltpu.VMEM((2, 128, HALF), BF16),
            pltpu.VMEM((2, 128, HALF), BF16),
            pltpu.VMEM((16, 16, HALF), BF16),
            dma((8,)),
            dma((8,)), dma((8,)), dma((8,)), dma((8,)), dma((4,)), dma((4,)),
            dma((16,)), dma((16,)), dma((16,)), dma((16,)), dma((3,)), dma((3,)),
            dma((3,)), dma((3,)), dma((2,)), dma((2,)), dma((16,)), dma((16,)),
        ],
        compiler_params=pltpu.CompilerParams(
            collective_id=0, has_side_effects=True, vmem_limit_bytes=int(53.8 * 2**20)),
        name="estep",
    )(particles, references, candidates.T, shifts.T, class_order.reshape(1, CLS))


def solution(mesh):
    return jax.shard_map(
        on_device,
        mesh=mesh,
        in_specs=(
            P(("blk", "grp"), None),
            P(("blk", "grp"), None),
            P(("blk", "grp"), None),
            P(),
            P(),
        ),
        out_specs=P("blk", "grp"),
        check_vma=False,
    )
```
